32 devices in a mesh: section: 4 (over x, core), dp: 8 (over z, y).
Axes of the slice: x: 2, y: 2, z: 4, core: 2. Of those that a mesh axis runs over, the one named last changes fastest.
Arguments:
- stack_input: bfloat16 [1024, 12288], P('dp'), may hold values from -6 to 6
- out_cotangent: bfloat16 [1024, 12288], P('dp'), may hold values from -6 to 6
- norm_gain: float32 [4, 12288], P('section'), may hold values from 0.5 to 1.5
- master_in: float32 [4, 12288, 128], P('section', 'dp'), may hold values from -0.0546875 to 0.0546875
- master_out: float32 [4, 128, 12288], P('section', None, 'dp'), may hold values from -0.5 to 0.5
- first_in: float32 [4, 12288, 128], P('section', 'dp'), may hold values from -3 to 3
- first_out: float32 [4, 128, 12288], P('section', None, 'dp'), may hold values from -0.1 to 0.1
- second_in: float32 [4, 12288, 128], P('section', 'dp'), may hold values from 0.02 to 0.5
- second_out: float32 [4, 128, 12288], P('section', None, 'dp'), may hold values from 0.02 to 0.5
Outputs:
- section_outputs: bfloat16 [4, 1024, 12288], P('section', 'dp')
- new_master_in: float32 [4, 12288, 128], P('section', 'dp')
- new_master_out: float32 [4, 128, 12288], P('section', None, 'dp')
- new_first_in: float32 [4, 12288, 128], P('section', 'dp')
- new_first_out: float32 [4, 128, 12288], P('section', None, 'dp')
- new_second_in: float32 [4, 12288, 128], P('section', 'dp')
- new_second_out: float32 [4, 128, 12288], P('section', None, 'dp')
The draws below stay inside these ranges and needn't reach their ends.
All inputs are finite; a program needn't handle non-finite values.
Results may differ from the reference program's by a relative error of at most 0.018.
Values may be sent and summed in bfloat16 or wider, within the bound.
A program may use at most 128 MiB of HBM per device.

```python
import math
import jax
import jax.numpy as jnp
from jax import lax

D = 12288
R = 128
STEP = 10
TOKENS = 1024
N_SECTION = 4


def block_levels(key, dims, pieces, smallest, top_value):
    def one(axis_at, shards_of):
        steps = jax.random.uniform(jax.random.fold_in(jax.random.fold_in(key, 6), axis_at), (shards_of,), jnp.float32, smallest / len(pieces), top_value / len(pieces))
        return jnp.repeat(jnp.exp(steps), dims[axis_at] // shards_of).reshape((-1,) + (1,) * (len(dims) - axis_at - 1))

    level = one(*pieces[0])
    for cut in pieces[1:]:
        level = level * one(*cut)
    return level


def noise(rng, shape, deviation, most, pieces=(), kind=jnp.bfloat16):
    entries = deviation * jax.random.normal(rng, shape, jnp.float32)
    if pieces:
        entries = entries * block_levels(rng, shape, pieces, -0.22, 0.18)
    return jnp.clip(entries, -most, most).astype(kind)


def setup_inputs(seed: int = 0) -> dict:
    keys = jax.random.split(jax.random.key(seed), 10)
    return {
        "stack_input": noise(keys[0], (TOKENS, D), 1.0, 6.0, ((0, 8),)),
        "out_cotangent": noise(keys[1], (TOKENS, D), 1.0, 6.0, ((0, 8),)),
        "norm_gain": jnp.clip(1.0 + 0.1 * jax.random.normal(keys[2], (N_SECTION, D), jnp.float32), 0.5, 1.5),
        "master_in": noise(keys[3], (N_SECTION, D, R), D ** -0.5, 0.0546875, ((0, 4), (1, 8)), jnp.float32),
        "master_out": noise(keys[4], (N_SECTION, R, D), R ** -0.5, 0.5, ((0, 4), (2, 8)), jnp.float32),
        "first_in": noise(keys[5], (N_SECTION, D, R), 0.5, 3.0, ((0, 4), (1, 8)), jnp.float32),
        "first_out": noise(keys[6], (N_SECTION, R, D), 0.02, 0.1, ((0, 4), (2, 8)), jnp.float32),
        "second_in": jnp.clip(jnp.exp(math.log(0.5) - 3.218876 * jax.random.uniform(keys[7], (N_SECTION, D, R), jnp.float32) ** block_levels(keys[7], (N_SECTION, D, R), ((0, 4), (1, 8)), -0.2, 0.2)), 0.02, 0.5),
        "second_out": jnp.clip(jnp.exp(math.log(0.5) - 3.218876 * jax.random.uniform(keys[8], (N_SECTION, R, D), jnp.float32) ** block_levels(keys[8], (N_SECTION, R, D), ((0, 4), (2, 8)), -0.2, 0.2)), 0.02, 0.5),
    }


norm_eps = 1e-05
gelu_coef = 0.7978845608028654
beta_one = 0.9
beta_two = 0.95
adam_eps = 1e-08
learn_rate = 0.05
decay_rate = 0.1
clip_rms = 0.5

def gelu_pair(hidden_pre):
    inner_arg = gelu_coef * (hidden_pre + 0.044715 * hidden_pre * hidden_pre * hidden_pre)
    tangent = jnp.tanh(inner_arg)
    gelu_value = 0.5 * hidden_pre * (1.0 + tangent)
    gelu_slope = 0.5 * (1.0 + tangent) + 0.5 * hidden_pre * (1.0 - tangent * tangent) * gelu_coef * (1.0 + 3.0 * 0.044715 * hidden_pre * hidden_pre)
    return (gelu_value, gelu_slope)

def contract_rows(left_arr, right_arr):
    return lax.dot_general(left_arr, right_arr, (((0,), (0,)), ((), ())), preferred_element_type=jnp.float32)

def contract_last(left_arr, right_arr):
    return lax.dot_general(left_arr, right_arr, (((1,), (1,)), ((), ())), preferred_element_type=jnp.float32)

def norm_parts(inputs, gain_row):
    wide_input = inputs.astype(jnp.float32)
    inv_rms = lax.rsqrt(lax.optimization_barrier(jnp.mean(wide_input * wide_input, axis=-1, keepdims=True)) + norm_eps)
    normed = (wide_input * inv_rms * gain_row).astype(jnp.bfloat16)
    return (wide_input, inv_rms, normed)

def layer_forward(inputs, gain_row, weight_in, weight_out):
    wide_input, inv_rms, normed = norm_parts(inputs, gain_row)
    hidden_pre = jnp.dot(normed, weight_in, preferred_element_type=jnp.float32)
    gelu_value, gelu_slope = gelu_pair(hidden_pre)
    act_low = gelu_value.astype(jnp.bfloat16)
    result = (wide_input + jnp.dot(act_low, weight_out, preferred_element_type=jnp.float32)).astype(jnp.bfloat16)
    return (result, hidden_pre)

def layer_backward(inputs, gain_row, weight_in, weight_out, hidden_pre, incoming):
    wide_input, inv_rms, normed = norm_parts(inputs, gain_row)
    gelu_value, gelu_slope = gelu_pair(hidden_pre)
    act_low = gelu_value.astype(jnp.bfloat16)
    d_act = contract_last(incoming, weight_out)
    d_pre = (d_act * gelu_slope).astype(jnp.bfloat16)
    scaled = contract_last(d_pre, weight_in) * gain_row
    d_inputs = incoming.astype(jnp.float32) + inv_rms * scaled - wide_input * inv_rms ** 3 * lax.optimization_barrier(jnp.mean(wide_input * scaled, axis=-1, keepdims=True))
    return (d_inputs.astype(jnp.bfloat16), d_pre, act_low, normed)

def adam_update(master, first, second, grad):
    first_new = beta_one * first + (1.0 - beta_one) * grad
    second_new = beta_two * second + (1.0 - beta_two) * grad * grad
    first_hat = first_new / (1.0 - beta_one ** STEP)
    second_hat = second_new / (1.0 - beta_two ** STEP)
    master_new = master - learn_rate * (first_hat / (jnp.sqrt(second_hat) + adam_eps) + decay_rate * master)
    return (master_new, first_new, second_new)

def reference(stack_input, out_cotangent, norm_gain, master_in, master_out, first_in, first_out, second_in, second_out):
    work_in = master_in.astype(jnp.bfloat16)
    work_out = master_out.astype(jnp.bfloat16)
    kept_inputs = []
    kept_pre = []
    outputs_list = []
    current = stack_input
    for section_num in range(N_SECTION):
        kept_inputs.append(current)
        current, hidden_pre = layer_forward(current, norm_gain[section_num], work_in[section_num], work_out[section_num])
        kept_pre.append(hidden_pre)
        outputs_list.append(current)
    incoming = out_cotangent
    grads_in = [None] * N_SECTION
    grads_out = [None] * N_SECTION
    for section_num in reversed(range(N_SECTION)):
        d_inputs, d_pre, act_low, normed = layer_backward(kept_inputs[section_num], norm_gain[section_num], work_in[section_num], work_out[section_num], kept_pre[section_num], incoming)
        grads_in[section_num] = contract_rows(normed, d_pre)
        grads_out[section_num] = contract_rows(act_low, incoming)
        incoming = d_inputs
    grad_in = jnp.stack(grads_in)
    grad_out = jnp.stack(grads_out)
    total_sq = jnp.sum(grad_in * grad_in) + jnp.sum(grad_out * grad_out)
    norm_limit = clip_rms * math.sqrt(2.0 * D * R * N_SECTION)
    clip_factor = norm_limit / jnp.maximum(jnp.sqrt(total_sq), norm_limit)
    new_in, new_first_in, new_second_in = adam_update(master_in, first_in, second_in, clip_factor * grad_in)
    new_out, new_first_out, new_second_out = adam_update(master_out, first_out, second_out, clip_factor * grad_out)
    return (jnp.stack(outputs_list), new_in, new_out, new_first_in, new_first_out, new_second_in, new_second_out)
```

```python
import functools
import math

import jax
import jax.numpy as jnp
from jax import lax
from jax.experimental import pallas as pl
from jax.experimental.pallas import tpu as pltpu
from jax.sharding import PartitionSpec as P

STEP = 10

norm_eps = 1e-05
gelu_coef = 0.7978845608028654
beta_one = 0.9
beta_two = 0.95
adam_eps = 1e-08
learn_rate = 0.05
decay_rate = 0.1
clip_rms = 0.5

BF16 = jnp.bfloat16
F32 = jnp.float32


def gelu_pair(hidden_pre):
    inner_arg = gelu_coef * (hidden_pre + 0.044715 * hidden_pre * hidden_pre * hidden_pre)
    tangent = jnp.tanh(inner_arg)
    gelu_value = 0.5 * hidden_pre * (1.0 + tangent)
    gelu_slope = 0.5 * (1.0 + tangent) + 0.5 * hidden_pre * (
        1.0 - tangent * tangent
    ) * gelu_coef * (1.0 + 3.0 * 0.044715 * hidden_pre * hidden_pre)
    return (gelu_value, gelu_slope)


def contract_rows(left_arr, right_arr):
    return lax.dot_general(
        left_arr, right_arr, (((0,), (0,)), ((), ())), preferred_element_type=F32
    )


def contract_last(left_arr, right_arr):
    return lax.dot_general(
        left_arr, right_arr, (((1,), (1,)), ((), ())), preferred_element_type=F32
    )


def adam_update(master, first, second, grad):
    first_new = beta_one * first + (1.0 - beta_one) * grad
    second_new = beta_two * second + (1.0 - beta_two) * grad * grad
    first_hat = first_new / (1.0 - beta_one**STEP)
    second_hat = second_new / (1.0 - beta_two**STEP)
    master_new = master - learn_rate * (
        first_hat / (jnp.sqrt(second_hat) + adam_eps) + decay_rate * master
    )
    return (master_new, first_new, second_new)


def split_halves(column, width):
    high = column.astype(BF16)
    low = (column - high.astype(F32)).astype(BF16)
    shape = (column.shape[0], width)
    return jnp.concatenate(
        [jnp.broadcast_to(high, shape), jnp.broadcast_to(low, shape)], axis=1
    )


def join_halves(values, rank):
    half = rank + rank // 2
    return values[:, rank : rank + 1].astype(F32) + values[:, half : half + 1].astype(F32)


def stack_kernel(
    S, DP, rb, F, R, D,
    x_hbm, cot_hbm, gain_hbm, win_hbm, wout_hbm,
    out_hbm, gin_ref, gout_ref, tot_ref,
    xs, cot, delta, gains, wi, wo,
    pay_f, rs_f, ag_f, pay_b, rs_b, ag_b,
    pre_keep, sum_keep, inv_keep,
    gi_send, go_send, gi_recv, go_recv, sq_send, sq_recv,
    x_send, x_recv, c_send, c_recv, gn_send, gn_recv,
    wi_ssem, wi_rsem, wo_ssem, wo_rsem,
    pf_s, pf_r, af_s, af_r, pb_s, pb_r, ab_s, ab_r,
    o_send, o_recv, g_send, g_recv, h_send, h_recv, q_send, q_recv,
):
    q = lax.axis_index("section")
    d = lax.axis_index("dp")
    N = S * DP
    T = DP * rb

    def place(sec, dp):
        return {"section": sec, "dp": dp}

    def send(src, dst, ssem, rsem, sec, dp):
        pltpu.make_async_remote_copy(
            src_ref=src, dst_ref=dst, send_sem=ssem, recv_sem=rsem,
            device_id=place(sec, dp), device_id_type=pl.DeviceIdType.MESH,
        ).start()

    def wait_bytes(ref, sem):
        pltpu.make_async_copy(ref, ref, sem).wait()

    def rows(block):
        return pl.ds(pl.multiple_of(block * rb, rb), rb)

    def cols(block):
        return pl.ds(pl.multiple_of(block * F, 128), F)

    me = q * DP + d
    barrier = pltpu.get_barrier_semaphore()

    def greet(j, carry):
        other = lax.rem(me + j, N)
        pl.semaphore_signal(
            barrier, inc=1, device_id=place(other // DP, lax.rem(other, DP)),
            device_id_type=pl.DeviceIdType.MESH,
        )
        return carry

    lax.fori_loop(1, N, greet, 0)
    pl.semaphore_wait(barrier, N - 1)

    def spread_rows(src_hbm, dst, ssem, rsem):
        def body(i, carry):
            peer = lax.rem(d + i, DP)
            send(src_hbm.at[rows(q), cols(peer)], dst.at[rows(d), :], ssem, rsem, q, peer)
            return carry

        lax.fori_loop(1, DP, body, 0)
        pltpu.make_async_copy(src_hbm.at[rows(q), cols(d)], dst.at[rows(d), :], rsem).start()

    def spread_layers(src, dst, ssem, rsem):
        for j in [S // 2] + [k for k in range(1, S) if k != S // 2]:
            send(src, dst.at[q], ssem, rsem.at[q], lax.rem(q + j, S), d)
        pltpu.make_async_copy(src, dst.at[q], rsem.at[q]).start()

    def exchange(src_of, dst, ssem, rsem):
        def body(i, carry):
            peer = lax.rem(d + i, DP)
            send(src_of(peer), dst.at[rows(d), :], ssem, rsem, q, peer)
            return carry

        lax.fori_loop(1, DP, body, 0)

    head = pl.ds(0, (DP - 1) * rb)

    spread_layers(gain_hbm.at[:, cols(d)], gains, gn_send, gn_recv)
    spread_rows(x_hbm, xs.at[pl.ds(0, T)], x_send, x_recv)
    spread_layers(win_hbm, wi, wi_ssem, wi_rsem)
    wait_bytes(xs.at[pl.ds(0, T)], x_recv)
    spread_layers(wout_hbm, wo, wo_ssem, wo_rsem)
    spread_rows(cot_hbm, cot, c_send, c_recv)

    def layer_rows(l):
        return pl.ds(l * T, T)

    def send_outputs(l):
        base = (l + 1) * T

        def block(peer):
            return xs.at[pl.ds(pl.multiple_of(base + peer * rb, rb), rb), :]

        def body(i, carry):
            peer = lax.rem(d + i, DP)
            send(block(peer), out_hbm.at[rows(q), cols(d)], o_send, o_recv, l, peer)
            return carry

        lax.fori_loop(1, DP, body, 0)

        @pl.when(q != l)
        def _():
            send(block(d), out_hbm.at[rows(q), cols(d)], o_send, o_recv, l, d)

        @pl.when(q == l)
        def _():
            pltpu.make_async_copy(block(d), out_hbm.at[rows(q), cols(d)], o_recv).start()

    for l in range(S):
        wait_bytes(gains.at[l], gn_recv.at[l])
        wait_bytes(wi.at[l], wi_rsem.at[l])
        wide = xs[layer_rows(l), :].astype(F32)
        part = jnp.dot((wide * gains[l]).astype(BF16), wi[l], preferred_element_type=F32)
        squares = jnp.sum(wide * wide, axis=1, keepdims=True)
        pay_f[l] = jnp.concatenate([part.astype(BF16), split_halves(squares, R // 2)], axis=1)
        exchange(lambda peer: pay_f.at[l, rows(peer), :], rs_f.at[l], pf_s.at[l], pf_r.at[l])
        rs_f[l, rows(d), :] = pay_f[l, rows(d), :]
        if l > 0:
            send_outputs(l - 1)
        wait_bytes(rs_f.at[l, head], pf_r.at[l])
        total = rs_f[l, 0:rb, :].astype(F32)
        for b in range(1, DP):
            total = total + rs_f[l, b * rb : (b + 1) * rb, :].astype(F32)
        inv = lax.rsqrt(join_halves(total, R) / D + norm_eps)
        pre = total[:, :R] * inv
        act, _ = gelu_pair(pre)
        pre_keep[l] = pre
        sum_keep[l] = total[:, :R]
        inv_keep[l] = jnp.broadcast_to(inv, (rb, R))
        ag_f[l, rows(d), :] = jnp.concatenate(
            [act.astype(BF16), split_halves(inv, R // 2)], axis=1
        )
        exchange(lambda peer: ag_f.at[l, rows(d), :], ag_f.at[l], af_s.at[l], af_r.at[l])
        wait_bytes(wo.at[l], wo_rsem.at[l])
        wait_bytes(ag_f.at[l, head], af_r.at[l])
        xs[layer_rows(l + 1), :] = (
            xs[layer_rows(l), :].astype(F32)
            + jnp.dot(ag_f[l, :, :R], wo[l], preferred_element_type=F32)
        ).astype(BF16)

    wait_bytes(cot, c_recv)

    def send_grads(l, incoming):
        normed = (
            xs[layer_rows(l), :].astype(F32) * join_halves(ag_f[l], R) * gains[l]
        ).astype(BF16)
        grad_in = contract_rows(normed, ag_b[l, :, :R])
        grad_out = contract_rows(ag_f[l, :, :R], incoming[...])

        @pl.when(q == l)
        def _():
            gin_ref[...] = grad_in
            gout_ref[...] = grad_out

        @pl.when(q != l)
        def _():
            gi_send[l] = grad_in.astype(BF16)
            go_send[l] = grad_out.astype(BF16)
            slot = lax.rem(q - l - 1 + 2 * S, S)
            send(gi_send.at[l], gi_recv.at[slot], g_send, g_recv, l, d)
            send(go_send.at[l], go_recv.at[slot], h_send, h_recv, l, d)

    for step in range(S):
        l = S - 1 - step
        incoming = cot if step == 0 else delta.at[step - 1]
        part = contract_last(incoming[...], wo[l])
        pay_b[l] = part.astype(BF16)
        exchange(lambda peer: pay_b.at[l, rows(peer), :], rs_b.at[l], pb_s.at[l], pb_r.at[l])
        rs_b[l, rows(d), :] = pay_b[l, rows(d), :]
        if step == 0:
            send_outputs(S - 1)
        else:
            send_grads(l + 1, cot if step == 1 else delta.at[step - 2])
        wait_bytes(rs_b.at[l, head], pb_r.at[l])
        total = rs_b[l, 0:rb, :].astype(F32)
        for b in range(1, DP):
            total = total + rs_b[l, b * rb : (b + 1) * rb, :].astype(F32)
        _, slope = gelu_pair(pre_keep[l])
        d_pre = (total * slope).astype(BF16)
        inv = inv_keep[l][:, 0:1]
        mean = jnp.sum(d_pre.astype(F32) * sum_keep[l], axis=1, keepdims=True) / D
        ag_b[l, rows(d), :] = jnp.concatenate(
            [d_pre, split_halves(inv * inv * inv * mean, R // 2)], axis=1
        )
        exchange(lambda peer: ag_b.at[l, rows(d), :], ag_b.at[l], ab_s.at[l], ab_r.at[l])
        wait_bytes(ag_b.at[l, head], ab_r.at[l])

        if l > 0:
            scaled = contract_last(ag_b[l, :, :R], wi[l]) * gains[l]
            delta[step] = (
                incoming[...].astype(F32)
                + join_halves(ag_f[l], R) * scaled
                - xs[layer_rows(l), :].astype(F32) * join_halves(ag_b[l], R)
            ).astype(BF16)

        if l == 0:
            send_grads(0, incoming)

    wait_bytes(gi_recv, g_recv)
    wait_bytes(go_recv, h_recv)
    grad_in = gin_ref[...]
    grad_out = gout_ref[...]
    for k in range(S - 1):
        grad_in = grad_in + gi_recv[k].astype(F32)
        grad_out = grad_out + go_recv[k].astype(F32)
    gin_ref[...] = grad_in
    gout_ref[...] = grad_out
    sq = jnp.sum((grad_in * grad_in).reshape(F // 8, 8, R), axis=0)
    sq_out = jnp.sum((grad_out * grad_out).reshape(R // 8, 8, F), axis=0)
    for k in range(F // 128):
        sq = sq + sq_out[:, k * 128 : (k + 1) * 128]
    sq_send[...] = sq

    def tell(j, carry):
        other = lax.rem(me + j, N)
        send(
            sq_send, sq_recv.at[pl.ds(pl.multiple_of((N - 1 - j) * 8, 8), 8), :],
            q_send, q_recv, other // DP, lax.rem(other, DP),
        )
        return carry

    lax.fori_loop(1, N, tell, 0)
    wait_bytes(sq_recv, q_recv)
    tot_ref[...] = sq + jnp.sum(sq_recv[...].reshape(N - 1, 8, 128), axis=0)

    wait_bytes(out_hbm, o_recv)
    wait_bytes(xs.at[pl.ds(0, (N - 1) * rb)], o_send)
    wait_bytes(xs.at[head], x_send)
    wait_bytes(xs.at[head], c_send)
    wait_bytes(gains.at[pl.ds(0, S - 1)], gn_send)
    wait_bytes(wi.at[pl.ds(0, S - 1)], wi_ssem)
    wait_bytes(wo.at[pl.ds(0, S - 1)], wo_ssem)
    wait_bytes(gi_recv, g_send)
    wait_bytes(go_recv, h_send)
    wait_bytes(sq_recv, q_send)
    for l in range(S):
        wait_bytes(rs_f.at[l, head], pf_s.at[l])
        wait_bytes(ag_f.at[l, head], af_s.at[l])
        wait_bytes(rs_b.at[l, head], pb_s.at[l])
        wait_bytes(ag_b.at[l, head], ab_s.at[l])


def run_stack(x, cot, gain, win, wout):
    S = lax.axis_size("section")
    DP = lax.axis_size("dp")
    tok, D = x.shape
    F, R = win.shape
    rb = tok // S
    T = DP * rb
    N = S * DP
    sem = pltpu.SemaphoreType.DMA
    any_spec = pl.BlockSpec(memory_space=pl.ANY)
    vmem_spec = pl.BlockSpec(memory_space=pltpu.VMEM)
    scratch = [
        pltpu.VMEM(((S + 1) * T, F), BF16),
        pltpu.VMEM((T, F), BF16),
        pltpu.VMEM((S, T, F), BF16),
        pltpu.VMEM((S, 1, F), F32),
        pltpu.VMEM((S, F, R), BF16),
        pltpu.VMEM((S, R, F), BF16),
        pltpu.VMEM((S, T, 2 * R), BF16),
        pltpu.VMEM((S, T, 2 * R), BF16),
        pltpu.VMEM((S, T, 2 * R), BF16),
        pltpu.VMEM((S, T, R), BF16),
        pltpu.VMEM((S, T, R), BF16),
        pltpu.VMEM((S, T, 2 * R), BF16),
        pltpu.VMEM((S, rb, R), F32),
        pltpu.VMEM((S, rb, R), F32),
        pltpu.VMEM((S, rb, R), F32),
        pltpu.VMEM((S, F, R), BF16),
        pltpu.VMEM((S, R, F), BF16),
        pltpu.VMEM((S - 1, F, R), BF16),
        pltpu.VMEM((S - 1, R, F), BF16),
        pltpu.VMEM((8, 128), F32),
        pltpu.VMEM(((N - 1) * 8, 128), F32),
        sem, sem, sem, sem, sem, sem((S,)),
        sem, sem((S,)), sem, sem((S,)),
        sem((S,)), sem((S,)), sem((S,)), sem((S,)),
        sem((S,)), sem((S,)), sem((S,)), sem((S,)),
        sem, sem, sem, sem, sem, sem, sem, sem,
    ]
    return pl.pallas_call(
        functools.partial(stack_kernel, S, DP, rb, F, R, D),
        out_shape=(
            jax.ShapeDtypeStruct((tok, D), BF16),
            jax.ShapeDtypeStruct((F, R), F32),
            jax.ShapeDtypeStruct((R, F), F32),
            jax.ShapeDtypeStruct((8, 128), F32),
        ),
        in_specs=[any_spec] * 5,
        out_specs=(any_spec, vmem_spec, vmem_spec, vmem_spec),
        scratch_shapes=scratch,
        compiler_params=pltpu.CompilerParams(
            collective_id=0, has_side_effects=True, vmem_limit_bytes=56 * 1024 * 1024
        ),
        name="adapter_stack",
    )(x, cot, gain, win, wout)


def shards(
    stack_input, out_cotangent, norm_gain, master_in, master_out,
    first_in, first_out, second_in, second_out,
):
    num_sections = lax.axis_size("section")
    model_width = stack_input.shape[1]
    rank_width = master_in.shape[2]
    section_rows, shard_in, shard_out, squares = run_stack(
        stack_input, out_cotangent, norm_gain,
        master_in[0].astype(BF16), master_out[0].astype(BF16),
    )
    total_sq = jnp.sum(squares)
    norm_limit = clip_rms * math.sqrt(2.0 * model_width * rank_width * num_sections)
    clip_factor = norm_limit / jnp.maximum(jnp.sqrt(total_sq), norm_limit)
    new_in, new_first_in, new_second_in = adam_update(
        master_in[0], first_in[0], second_in[0], clip_factor * shard_in
    )
    new_out, new_first_out, new_second_out = adam_update(
        master_out[0], first_out[0], second_out[0], clip_factor * shard_out
    )
    return (
        section_rows[None],
        new_in[None],
        new_out[None],
        new_first_in[None],
        new_first_out[None],
        new_second_in[None],
        new_second_out[None],
    )


def solution(mesh):
    in_specs = (
        P("dp", None),
        P("dp", None),
        P("section", None),
        P("section", "dp", None),
        P("section", None, "dp"),
        P("section", "dp", None),
        P("section", None, "dp"),
        P("section", "dp", None),
        P("section", None, "dp"),
    )
    out_specs = (
        P("section", "dp", None),
        P("section", "dp", None),
        P("section", None, "dp"),
        P("section", "dp", None),
        P("section", None, "dp"),
        P("section", "dp", None),
        P("section", None, "dp"),
    )
    return jax.shard_map(shards, mesh=mesh, in_specs=in_specs, out_specs=out_specs, check_vma=False)
```

```python
import functools
import math

import jax
import jax.numpy as jnp
from jax import lax
from jax.experimental import pallas as pl
from jax.experimental.pallas import tpu as pltpu
from jax.sharding import PartitionSpec as P

STEP = 10

norm_eps = 1e-05
gelu_coef = 0.7978845608028654
beta_one = 0.9
beta_two = 0.95
adam_eps = 1e-08
learn_rate = 0.05
decay_rate = 0.1
clip_rms = 0.5

BF16 = jnp.bfloat16
F32 = jnp.float32


def gelu_pair(hidden_pre):
    inner_arg = gelu_coef * (hidden_pre + 0.044715 * hidden_pre * hidden_pre * hidden_pre)
    tangent = jnp.tanh(inner_arg)
    gelu_value = 0.5 * hidden_pre * (1.0 + tangent)
    gelu_slope = 0.5 * (1.0 + tangent) + 0.5 * hidden_pre * (
        1.0 - tangent * tangent
    ) * gelu_coef * (1.0 + 3.0 * 0.044715 * hidden_pre * hidden_pre)
    return (gelu_value, gelu_slope)


def contract_rows(left_arr, right_arr):
    return lax.dot_general(
        left_arr, right_arr, (((0,), (0,)), ((), ())), preferred_element_type=F32
    )


def contract_last(left_arr, right_arr):
    return lax.dot_general(
        left_arr, right_arr, (((1,), (1,)), ((), ())), preferred_element_type=F32
    )


def adam_update(master, first, second, grad):
    first_new = beta_one * first + (1.0 - beta_one) * grad
    second_new = beta_two * second + (1.0 - beta_two) * grad * grad
    first_hat = first_new / (1.0 - beta_one**STEP)
    second_hat = second_new / (1.0 - beta_two**STEP)
    master_new = master - learn_rate * (
        first_hat / (jnp.sqrt(second_hat) + adam_eps) + decay_rate * master
    )
    return (master_new, first_new, second_new)


def split_halves(column, width):
    high = column.astype(BF16)
    low = (column - high.astype(F32)).astype(BF16)
    shape = (column.shape[0], width)
    return jnp.concatenate(
        [jnp.broadcast_to(high, shape), jnp.broadcast_to(low, shape)], axis=1
    )


def join_halves(values, start, width):
    high = values[:, start : start + 1].astype(F32)
    return high + values[:, start + width : start + width + 1].astype(F32)


def stack_kernel(
    S, DP, rb, F, R, D,
    x_hbm, cot_hbm, gain_hbm, win_ref, wout_ref,
    out_hbm, gin_ref, gout_ref, tot_ref,
    xs, cot, delta, gains, wi, wo,
    pay_f, rs_f, ag_f, pay_b, rs_b, ag_b,
    pre_keep, sum_keep, inv_keep,
    gi_send, go_send, gi_recv, go_recv, sq_send, sq_recv,
    x_send, x_recv, c_send, c_recv, gn_send, gn_recv,
    wi_ssem, wi_rsem, wo_ssem, wo_rsem,
    pf_s, pf_r, af_s, af_r, pb_s, pb_r, ab_s, ab_r,
    o_send, o_recv, g_send, g_recv, h_send, h_recv, q_send, q_recv,
):
    q = lax.axis_index("section")
    d = lax.axis_index("dp")
    N = S * DP
    T = DP * rb

    def place(sec, dp):
        return {"section": sec, "dp": dp}

    def send(src, dst, ssem, rsem, sec, dp):
        pltpu.make_async_remote_copy(
            src_ref=src, dst_ref=dst, send_sem=ssem, recv_sem=rsem,
            device_id=place(sec, dp), device_id_type=pl.DeviceIdType.MESH,
        ).start()

    def wait_bytes(ref, sem):
        pltpu.make_async_copy(ref, ref, sem).wait()

    def rows(block):
        return pl.ds(pl.multiple_of(block * rb, rb), rb)

    def cols(block):
        return pl.ds(pl.multiple_of(block * F, 128), F)

    me = q * DP + d
    barrier = pltpu.get_barrier_semaphore()

    def greet(j, carry):
        other = lax.rem(me + j, N)
        pl.semaphore_signal(
            barrier, inc=1, device_id=place(other // DP, lax.rem(other, DP)),
            device_id_type=pl.DeviceIdType.MESH,
        )
        return carry

    lax.fori_loop(1, N, greet, 0)
    own_gain = pltpu.make_async_copy(gain_hbm.at[:, cols(d)], gains.at[q], gn_recv.at[q])
    own_gain.start()
    wi[q] = win_ref[...].astype(BF16)
    wo[q] = wout_ref[...].astype(BF16)
    own_gain.wait()
    pl.semaphore_wait(barrier, N - 1)

    def send_rows(i, src_hbm, dst, ssem, rsem):
        if i == 0:
            pltpu.make_async_copy(src_hbm.at[rows(q), cols(d)], dst.at[rows(d), :], rsem).start()
        else:
            peer = lax.rem(d + i, DP)
            send(src_hbm.at[rows(q), cols(peer)], dst.at[rows(d), :], ssem, rsem, q, peer)

    def spread_layers(src, dst, ssem, rsem):
        for j in [S // 2] + [k for k in range(1, S) if k != S // 2]:
            send(src, dst.at[q], ssem, rsem.at[q], lax.rem(q + j, S), d)

    def wait_layer(buffer, rsem, l):
        @pl.when(q != l)
        def _():
            wait_bytes(buffer.at[l], rsem.at[l])

    def exchange(src_of, dst, ssem, rsem):
        def body(i, carry):
            peer = lax.rem(d + i, DP)
            send(src_of(peer), dst.at[rows(d), :], ssem, rsem, q, peer)
            return carry

        lax.fori_loop(1, DP, body, 0)

    head = pl.ds(0, (DP - 1) * rb)

    for i in range(DP):
        send_rows(i, x_hbm, xs.at[pl.ds(0, T)], x_send, x_recv)
    spread_layers(gains.at[q], gains, gn_send, gn_recv)
    spread_layers(wi.at[q], wi, wi_ssem, wi_rsem)
    wait_bytes(xs.at[pl.ds(0, T)], x_recv)
    spread_layers(wo.at[q], wo, wo_ssem, wo_rsem)

    def layer_rows(l):
        return pl.ds(l * T, T)

    def send_output(l, i):
        peer = lax.rem(d + i, DP)
        block = xs.at[pl.ds(pl.multiple_of((l + 1) * T + peer * rb, rb), rb), :]
        target = out_hbm.at[rows(q), cols(d)]
        if i > 0:
            send(block, target, o_send, o_recv, l, peer)
            return

        @pl.when(q != l)
        def _():
            send(block, target, o_send, o_recv, l, peer)

        @pl.when(q == l)
        def _():
            pltpu.make_async_copy(block, target, o_recv).start()

    waiting_cot = list(range(DP))
    waiting_out = []

    def send_some_cot(count):
        for _ in range(min(count, len(waiting_cot))):
            send_rows(waiting_cot.pop(0), cot_hbm, cot, c_send, c_recv)

    def send_some_out(count):
        for _ in range(min(count, len(waiting_out))):
            send_output(*waiting_out.pop(0))

    def send_bulk():
        if waiting_cot:
            send_some_cot(-(-DP // 4))
        else:
            send_some_out(-(-DP * S // (3 * S - 1)))

    for l in range(S):
        wait_layer(gains, gn_recv, l)
        wait_layer(wi, wi_rsem, l)
        wide = xs[layer_rows(l), :].astype(F32)
        part = jnp.dot((wide * gains[l]).astype(BF16), wi[l], preferred_element_type=F32)
        squares = jnp.sum(wide * wide, axis=1, keepdims=True)
        pay_f[l] = jnp.concatenate([part.astype(BF16), split_halves(squares, R // 2)], axis=1)
        exchange(lambda peer: pay_f.at[l, rows(peer), :], rs_f.at[l], pf_s.at[l], pf_r.at[l])
        rs_f[l, rows(d), :] = pay_f[l, rows(d), :]
        send_bulk()
        wait_bytes(rs_f.at[l, head], pf_r.at[l])
        total = rs_f[l, 0:rb, :].astype(F32)
        for b in range(1, DP):
            total = total + rs_f[l, b * rb : (b + 1) * rb, :].astype(F32)
        inv = lax.rsqrt(join_halves(total, R, R // 2) / D + norm_eps)
        pre = total[:, :R] * inv
        act, _ = gelu_pair(pre)
        pre_keep[l] = pre
        sum_keep[l] = total[:, :R]
        inv_keep[l] = jnp.broadcast_to(inv, (rb, R))
        ag_f[l, rows(d), :] = act.astype(BF16)
        exchange(lambda peer: ag_f.at[l, rows(d), :], ag_f.at[l], af_s.at[l], af_r.at[l])
        send_bulk()
        wait_layer(wo, wo_rsem, l)
        wait_bytes(ag_f.at[l, head], af_r.at[l])
        xs[layer_rows(l + 1), :] = (
            xs[layer_rows(l), :].astype(F32)
            + jnp.dot(ag_f[l], wo[l], preferred_element_type=F32)
        ).astype(BF16)
        waiting_out.extend((l, i) for i in range(DP))

    send_some_cot(DP)
    wait_bytes(cot, c_recv)

    def pass_grad(l, grad, own, outgoing, arriving, ssem, rsem):
        @pl.when(q == l)
        def _():
            own[...] = grad

        @pl.when(q != l)
        def _():
            outgoing[l] = grad.astype(BF16)
            slot = lax.rem(q - l - 1 + 2 * S, S)
            send(outgoing.at[l], arriving.at[slot], ssem, rsem, l, d)

    def send_grad_in(l):
        inv = join_halves(ag_b[l], R + R // 2, R // 4)
        normed = (xs[layer_rows(l), :].astype(F32) * inv * gains[l]).astype(BF16)
        grad_in = contract_rows(normed, ag_b[l, :, :R])
        pass_grad(l, grad_in, gin_ref, gi_send, gi_recv, g_send, g_recv)

    def send_grad_out(l, incoming):
        grad_out = contract_rows(ag_f[l], incoming[...])
        pass_grad(l, grad_out, gout_ref, go_send, go_recv, h_send, h_recv)

    for step in range(S):
        l = S - 1 - step
        incoming = cot if step == 0 else delta.at[step - 1]
        part = contract_last(incoming[...], wo[l])
        pay_b[l] = part.astype(BF16)
        exchange(lambda peer: pay_b.at[l, rows(peer), :], rs_b.at[l], pb_s.at[l], pb_r.at[l])
        rs_b[l, rows(d), :] = pay_b[l, rows(d), :]
        send_bulk()
        send_grad_out(l, incoming)
        if step > 0:
            send_grad_in(l + 1)
        wait_bytes(rs_b.at[l, head], pb_r.at[l])
        total = rs_b[l, 0:rb, :].astype(F32)
        for b in range(1, DP):
            total = total + rs_b[l, b * rb : (b + 1) * rb, :].astype(F32)
        _, slope = gelu_pair(pre_keep[l])
        d_pre = (total * slope).astype(BF16)
        inv = inv_keep[l][:, 0:1]
        mean = jnp.sum(d_pre.astype(F32) * sum_keep[l], axis=1, keepdims=True) / D
        ag_b[l, rows(d), :] = jnp.concatenate(
            [d_pre, split_halves(inv * inv * inv * mean, R // 4), split_halves(inv, R // 4)],
            axis=1,
        )
        exchange(lambda peer: ag_b.at[l, rows(d), :], ag_b.at[l], ab_s.at[l], ab_r.at[l])
        send_bulk()
        wait_bytes(ag_b.at[l, head], ab_r.at[l])

        if l > 0:
            scaled = contract_last(ag_b[l, :, :R], wi[l]) * gains[l]
            delta[step] = (
                incoming[...].astype(F32)
                + join_halves(ag_b[l], R + R // 2, R // 4) * scaled
                - xs[layer_rows(l), :].astype(F32) * join_halves(ag_b[l], R, R // 4)
            ).astype(BF16)

        if l == 0:
            send_grad_in(0)
            send_some_out(len(waiting_out))

    wait_bytes(gi_recv, g_recv)
    wait_bytes(go_recv, h_recv)
    grad_in = gin_ref[...]
    grad_out = gout_ref[...]
    for k in range(S - 1):
        grad_in = grad_in + gi_recv[k].astype(F32)
        grad_out = grad_out + go_recv[k].astype(F32)
    gin_ref[...] = grad_in
    gout_ref[...] = grad_out
    sq = jnp.sum((grad_in * grad_in).reshape(F // 8, 8, R), axis=0)
    sq_out = jnp.sum((grad_out * grad_out).reshape(R // 8, 8, F), axis=0)
    for k in range(F // 128):
        sq = sq + sq_out[:, k * 128 : (k + 1) * 128]
    sq_send[...] = sq

    def tell(j, carry):
        other = lax.rem(me + j, N)
        send(
            sq_send, sq_recv.at[pl.ds(pl.multiple_of((N - 1 - j) * 8, 8), 8), :],
            q_send, q_recv, other // DP, lax.rem(other, DP),
        )
        return carry

    lax.fori_loop(1, N, tell, 0)
    wait_bytes(sq_recv, q_recv)
    tot_ref[...] = sq + jnp.sum(sq_recv[...].reshape(N - 1, 8, 128), axis=0)

    wait_bytes(out_hbm, o_recv)
    wait_bytes(xs.at[pl.ds(0, (N - 1) * rb)], o_send)
    wait_bytes(xs.at[head], x_send)
    wait_bytes(xs.at[head], c_send)
    wait_bytes(gains.at[pl.ds(0, S - 1)], gn_send)
    wait_bytes(wi.at[pl.ds(0, S - 1)], wi_ssem)
    wait_bytes(wo.at[pl.ds(0, S - 1)], wo_ssem)
    wait_bytes(gi_recv, g_send)
    wait_bytes(go_recv, h_send)
    wait_bytes(sq_recv, q_send)
    for l in range(S):
        wait_bytes(rs_f.at[l, head], pf_s.at[l])
        wait_bytes(ag_f.at[l, head], af_s.at[l])
        wait_bytes(rs_b.at[l, head], pb_s.at[l])
        wait_bytes(ag_b.at[l, head], ab_s.at[l])


def run_stack(x, cot, gain, win, wout):
    S = lax.axis_size("section")
    DP = lax.axis_size("dp")
    tok, D = x.shape
    F, R = win.shape
    rb = tok // S
    T = DP * rb
    N = S * DP
    sem = pltpu.SemaphoreType.DMA
    any_spec = pl.BlockSpec(memory_space=pl.ANY)
    vmem_spec = pl.BlockSpec(memory_space=pltpu.VMEM)
    scratch = [
        pltpu.VMEM(((S + 1) * T, F), BF16),
        pltpu.VMEM((T, F), BF16),
        pltpu.VMEM((S, T, F), BF16),
        pltpu.VMEM((S, 1, F), F32),
        pltpu.VMEM((S, F, R), BF16),
        pltpu.VMEM((S, R, F), BF16),
        pltpu.VMEM((S, T, 2 * R), BF16),
        pltpu.VMEM((S, T, 2 * R), BF16),
        pltpu.VMEM((S, T, R), BF16),
        pltpu.VMEM((S, T, R), BF16),
        pltpu.VMEM((S, T, R), BF16),
        pltpu.VMEM((S, T, 2 * R), BF16),
        pltpu.VMEM((S, rb, R), F32),
        pltpu.VMEM((S, rb, R), F32),
        pltpu.VMEM((S, rb, R), F32),
        pltpu.VMEM((S, F, R), BF16),
        pltpu.VMEM((S, R, F), BF16),
        pltpu.VMEM((S - 1, F, R), BF16),
        pltpu.VMEM((S - 1, R, F), BF16),
        pltpu.VMEM((8, 128), F32),
        pltpu.VMEM(((N - 1) * 8, 128), F32),
        sem, sem, sem, sem, sem, sem((S,)),
        sem, sem((S,)), sem, sem((S,)),
        sem((S,)), sem((S,)), sem((S,)), sem((S,)),
        sem((S,)), sem((S,)), sem((S,)), sem((S,)),
        sem, sem, sem, sem, sem, sem, sem, sem,
    ]
    return pl.pallas_call(
        functools.partial(stack_kernel, S, DP, rb, F, R, D),
        out_shape=(
            jax.ShapeDtypeStruct((tok, D), BF16),
            jax.ShapeDtypeStruct((F, R), F32),
            jax.ShapeDtypeStruct((R, F), F32),
            jax.ShapeDtypeStruct((8, 128), F32),
        ),
        in_specs=[any_spec] * 3 + [vmem_spec] * 2,
        out_specs=(any_spec, vmem_spec, vmem_spec, vmem_spec),
        scratch_shapes=scratch,
        compiler_params=pltpu.CompilerParams(
            collective_id=0, has_side_effects=True, vmem_limit_bytes=56 * 1024 * 1024
        ),
        name="adapter_stack",
    )(x, cot, gain, win, wout)


def shards(
    stack_input, out_cotangent, norm_gain, master_in, master_out,
    first_in, first_out, second_in, second_out,
):
    num_sections = lax.axis_size("section")
    model_width = stack_input.shape[1]
    rank_width = master_in.shape[2]
    section_rows, shard_in, shard_out, squares = run_stack(
        stack_input, out_cotangent, norm_gain,
        master_in[0], master_out[0],
    )
    total_sq = jnp.sum(squares)
    norm_limit = clip_rms * math.sqrt(2.0 * model_width * rank_width * num_sections)
    clip_factor = norm_limit / jnp.maximum(jnp.sqrt(total_sq), norm_limit)
    new_in, new_first_in, new_second_in = adam_update(
        master_in[0], first_in[0], second_in[0], clip_factor * shard_in
    )
    new_out, new_first_out, new_second_out = adam_update(
        master_out[0], first_out[0], second_out[0], clip_factor * shard_out
    )
    return (
        section_rows[None],
        new_in[None],
        new_out[None],
        new_first_in[None],
        new_first_out[None],
        new_second_in[None],
        new_second_out[None],
    )


def solution(mesh):
    in_specs = (
        P("dp", None),
        P("dp", None),
        P("section", None),
        P("section", "dp", None),
        P("section", None, "dp"),
        P("section", "dp", None),
        P("section", None, "dp"),
        P("section", "dp", None),
        P("section", None, "dp"),
    )
    out_specs = (
        P("section", "dp", None),
        P("section", "dp", None),
        P("section", None, "dp"),
        P("section", "dp", None),
        P("section", None, "dp"),
        P("section", "dp", None),
        P("section", None, "dp"),
    )
    return jax.shard_map(shards, mesh=mesh, in_specs=in_specs, out_specs=out_specs, check_vma=False)
```

```python
import functools
import math

import jax
import jax.numpy as jnp
from jax import lax
from jax.experimental import pallas as pl
from jax.experimental.pallas import tpu as pltpu
from jax.sharding import PartitionSpec as P

STEP = 10

norm_eps = 1e-05
gelu_coef = 0.7978845608028654
beta_one = 0.9
beta_two = 0.95
adam_eps = 1e-08
learn_rate = 0.05
decay_rate = 0.1
clip_rms = 0.5

BF16 = jnp.bfloat16
F32 = jnp.float32


def gelu_pair(hidden_pre):
    inner_arg = gelu_coef * (hidden_pre + 0.044715 * hidden_pre * hidden_pre * hidden_pre)
    tangent = jnp.tanh(inner_arg)
    gelu_value = 0.5 * hidden_pre * (1.0 + tangent)
    gelu_slope = 0.5 * (1.0 + tangent) + 0.5 * hidden_pre * (
        1.0 - tangent * tangent
    ) * gelu_coef * (1.0 + 3.0 * 0.044715 * hidden_pre * hidden_pre)
    return (gelu_value, gelu_slope)


def contract_rows(left_arr, right_arr):
    return lax.dot_general(
        left_arr, right_arr, (((0,), (0,)), ((), ())), preferred_element_type=F32
    )


def contract_last(left_arr, right_arr):
    return lax.dot_general(
        left_arr, right_arr, (((1,), (1,)), ((), ())), preferred_element_type=F32
    )


def adam_update(master, first, second, grad):
    first_new = beta_one * first + (1.0 - beta_one) * grad
    second_new = beta_two * second + (1.0 - beta_two) * grad * grad
    first_hat = first_new / (1.0 - beta_one**STEP)
    second_hat = second_new / (1.0 - beta_two**STEP)
    master_new = master - learn_rate * (
        first_hat / (jnp.sqrt(second_hat) + adam_eps) + decay_rate * master
    )
    return (master_new, first_new, second_new)


def split_halves(column, width):
    high = column.astype(BF16)
    low = (column - high.astype(F32)).astype(BF16)
    shape = (column.shape[0], width)
    return jnp.concatenate(
        [jnp.broadcast_to(high, shape), jnp.broadcast_to(low, shape)], axis=1
    )


def join_halves(values, start, width):
    high = values[:, start : start + 1].astype(F32)
    return high + values[:, start + width : start + width + 1].astype(F32)


def stack_kernel(
    S, DP, H, rb, F, R, D,
    x_hbm, cot_hbm, gain_hbm, win_ref, wout_ref,
    out_hbm, gin_ref, gout_ref, tot_ref,
    xs, cot, delta, gains, wi, wo,
    pay_f, rs_f, ag_f, pay_b, rs_b, ag_b,
    pre_keep, sum_keep, inv_keep,
    gi_send, go_send, gi_recv, go_recv, sq_send, sq_recv,
    x_send, x_recv, c_send, c_recv, gn_send, gn_recv,
    wi_ssem, wi_rsem, wo_ssem, wo_rsem,
    pf_s, pf_r, af_s, af_r, pb_s, pb_r, ab_s, ab_r,
    o_send, o_recv, g_send, g_recv, h_send, h_recv, q_send, q_recv,
):
    q = lax.axis_index("section")
    d = lax.axis_index("dp")
    N = S * DP
    T = DP * rb
    rh = rb // H
    Th = DP * rh

    def place(sec, dp):
        return {"section": sec, "dp": dp}

    def send(src, dst, ssem, rsem, sec, dp):
        pltpu.make_async_remote_copy(
            src_ref=src, dst_ref=dst, send_sem=ssem, recv_sem=rsem,
            device_id=place(sec, dp), device_id_type=pl.DeviceIdType.MESH,
        ).start()

    def wait_bytes(ref, sem):
        pltpu.make_async_copy(ref, ref, sem).wait()

    def home_rows(h):
        return pl.ds(pl.multiple_of(q * rb + h * rh, rh), rh)

    def rows(block, h=0, base=0):
        return pl.ds(pl.multiple_of(base + h * Th + block * rh, rh), rh)

    def cols(block):
        return pl.ds(pl.multiple_of(block * F, 128), F)

    me = q * DP + d
    barrier = pltpu.get_barrier_semaphore()

    def greet(j, carry):
        other = lax.rem(me + j, N)
        pl.semaphore_signal(
            barrier, inc=1, device_id=place(other // DP, lax.rem(other, DP)),
            device_id_type=pl.DeviceIdType.MESH,
        )
        return carry

    lax.fori_loop(1, N, greet, 0)
    own_gain = pltpu.make_async_copy(gain_hbm.at[:, cols(d)], gains.at[q], gn_recv.at[q])
    own_gain.start()
    wi[q] = win_ref[...].astype(BF16)
    wo[q] = wout_ref[...].astype(BF16)
    own_gain.wait()
    pl.semaphore_wait(barrier, N - 1)

    def send_rows(h, i, src_hbm, dst, ssem, rsem):
        target = dst.at[rows(d, h), :]
        if i == 0:
            src = src_hbm.at[home_rows(h), cols(d)]
            pltpu.make_async_copy(src, target, rsem.at[h]).start()
        else:
            peer = lax.rem(d + i, DP)
            src = src_hbm.at[home_rows(h), cols(peer)]
            send(src, target, ssem.at[h], rsem.at[h], q, peer)

    def spread_layers(src, dst, ssem, rsem):
        for j in [S // 2] + [k for k in range(1, S) if k != S // 2]:
            send(src, dst.at[q], ssem, rsem.at[q], lax.rem(q + j, S), d)

    def wait_layer(buffer, rsem, l):
        @pl.when(q != l)
        def _():
            wait_bytes(buffer.at[l], rsem.at[l])

    def exchange(src_of, target, ssem, rsem):
        def body(i, carry):
            peer = lax.rem(d + i, DP)
            send(src_of(peer), target, ssem, rsem, q, peer)
            return carry

        lax.fori_loop(1, DP, body, 0)

    head = pl.ds(0, (DP - 1) * rh)

    for h in range(H):
        for i in range(DP):
            send_rows(h, i, x_hbm, xs.at[pl.ds(0, T)], x_send, x_recv)
        if h == 0:
            spread_layers(gains.at[q], gains, gn_send, gn_recv)
            spread_layers(wi.at[q], wi, wi_ssem, wi_rsem)

    def layer_rows(l):
        return pl.ds(l * T, T)

    def stream_rows(h, l=0):
        return pl.ds(l * T + h * Th, Th)

    def send_output(l, h, i):
        peer = lax.rem(d + i, DP)
        block = xs.at[rows(peer, h, (l + 1) * T), :]
        target = out_hbm.at[home_rows(h), cols(d)]
        if i > 0:
            send(block, target, o_send, o_recv, l, peer)
            return

        @pl.when(q != l)
        def _():
            send(block, target, o_send, o_recv, l, peer)

        @pl.when(q == l)
        def _():
            pltpu.make_async_copy(block, target, o_recv).start()

    waiting_cot = [(h, i) for h in range(H) for i in range(DP)]
    waiting_out = []

    def send_some_cot(count):
        for _ in range(min(count, len(waiting_cot))):
            send_rows(*waiting_cot.pop(0), cot_hbm, cot, c_send, c_recv)

    def send_some_out(count):
        for _ in range(min(count, len(waiting_out))):
            send_output(*waiting_out.pop(0))

    def send_bulk():
        if waiting_cot:
            send_some_cot(-(-DP // S))
        else:
            send_some_out(-(-DP // 3))

    def add_blocks(buffer, k):
        total = buffer[k, 0:rh, :].astype(F32)
        for b in range(1, DP):
            total = total + buffer[k, b * rh : (b + 1) * rh, :].astype(F32)
        return total

    def forward_partial(l, h):
        k = l * H + h
        if l == 0:
            wait_bytes(xs.at[stream_rows(h)], x_recv.at[h])
        if h == 0:
            wait_layer(gains, gn_recv, l)
            wait_layer(wi, wi_rsem, l)
        wide = xs[stream_rows(h, l), :].astype(F32)
        part = jnp.dot((wide * gains[l]).astype(BF16), wi[l], preferred_element_type=F32)
        squares = jnp.sum(wide * wide, axis=1, keepdims=True)
        pay_f[k] = jnp.concatenate([part.astype(BF16), split_halves(squares, R // 2)], axis=1)
        exchange(
            lambda peer: pay_f.at[k, rows(peer), :], rs_f.at[k, rows(d), :], pf_s.at[k], pf_r.at[k]
        )
        rs_f[k, rows(d), :] = pay_f[k, rows(d), :]

    def forward_act(l, h):
        k = l * H + h
        wait_bytes(rs_f.at[k, head], pf_r.at[k])
        total = add_blocks(rs_f, k)
        inv = lax.rsqrt(join_halves(total, R, R // 2) / D + norm_eps)
        pre = total[:, :R] * inv
        act, _ = gelu_pair(pre)
        mine = ag_f.at[l, rows(d, h), :]
        mine[...] = act.astype(BF16)
        exchange(lambda peer: mine, mine, af_s.at[k], af_r.at[k])
        pre_keep[k] = pre
        sum_keep[k] = total[:, :R]
        inv_keep[k] = jnp.broadcast_to(inv, (rh, R))

    def forward_add(l, h):
        k = l * H + h
        if h == 0:
            wait_layer(wo, wo_rsem, l)
        wait_bytes(ag_f.at[l, head], af_r.at[k])
        xs[stream_rows(h, l + 1), :] = (
            xs[stream_rows(h, l), :].astype(F32)
            + jnp.dot(ag_f[l, stream_rows(h), :], wo[l], preferred_element_type=F32)
        ).astype(BF16)
        waiting_out.extend((l, h, i) for i in range(DP))

    for h in range(H):
        forward_partial(0, h)
        if h == 0:
            spread_layers(wo.at[q], wo, wo_ssem, wo_rsem)
        send_bulk()
    for l in range(S):
        for h in range(H):
            forward_act(l, h)
            send_bulk()
        for h in range(H):
            forward_add(l, h)
            if l + 1 < S:
                forward_partial(l + 1, h)
                send_bulk()

    send_some_cot(DP * H)

    def pass_grad(l, grad, own, outgoing, arriving, ssem, rsem):
        @pl.when(q == l)
        def _():
            own[...] = grad

        @pl.when(q != l)
        def _():
            outgoing[l] = grad.astype(BF16)
            slot = lax.rem(q - l - 1 + 2 * S, S)
            send(outgoing.at[l], arriving.at[slot], ssem, rsem, l, d)

    def send_grad_in(l):
        inv = join_halves(ag_b[l], R + R // 2, R // 4)
        normed = (xs[layer_rows(l), :].astype(F32) * inv * gains[l]).astype(BF16)
        grad_in = contract_rows(normed, ag_b[l, :, :R])
        pass_grad(l, grad_in, gin_ref, gi_send, gi_recv, g_send, g_recv)

    def send_grad_out(l, incoming):
        grad_out = contract_rows(ag_f[l], incoming[...])
        pass_grad(l, grad_out, gout_ref, go_send, go_recv, h_send, h_recv)

    def incoming(l):
        return cot if l == S - 1 else delta.at[l]

    def backward_partial(l, h):
        k = l * H + h
        if l == S - 1:
            wait_bytes(cot.at[stream_rows(h)], c_recv.at[h])
        part = contract_last(incoming(l)[stream_rows(h), :], wo[l])
        pay_b[k] = part.astype(BF16)
        exchange(
            lambda peer: pay_b.at[k, rows(peer), :], rs_b.at[k, rows(d), :], pb_s.at[k], pb_r.at[k]
        )
        rs_b[k, rows(d), :] = pay_b[k, rows(d), :]

    def backward_slope(l, h):
        k = l * H + h
        _, slope = gelu_pair(pre_keep[k])
        inv = inv_keep[k][:, 0:1]
        wait_bytes(rs_b.at[k, head], pb_r.at[k])
        d_pre = (add_blocks(rs_b, k) * slope).astype(BF16)
        mean = jnp.sum(d_pre.astype(F32) * sum_keep[k], axis=1, keepdims=True) / D
        mine = ag_b.at[l, rows(d, h), :]
        mine[...] = jnp.concatenate(
            [d_pre, split_halves(inv * inv * inv * mean, R // 4), split_halves(inv, R // 4)],
            axis=1,
        )
        exchange(lambda peer: mine, mine, ab_s.at[k], ab_r.at[k])

    def backward_add(l, h):
        wait_bytes(ag_b.at[l, head], ab_r.at[l * H + h])
        if l == 0:
            return
        gathered = ag_b[l, stream_rows(h), :]
        scaled = contract_last(gathered[:, :R], wi[l]) * gains[l]
        delta[l - 1, stream_rows(h), :] = (
            incoming(l)[stream_rows(h), :].astype(F32)
            + join_halves(gathered, R + R // 2, R // 4) * scaled
            - xs[stream_rows(h, l), :].astype(F32) * join_halves(gathered, R, R // 4)
        ).astype(BF16)

    for h in range(H):
        backward_partial(S - 1, h)
        send_bulk()
    for l in range(S - 1, -1, -1):
        send_grad_out(l, incoming(l))
        for h in range(H):
            backward_slope(l, h)
            send_bulk()
        if l + 1 < S:
            send_grad_in(l + 1)
        for h in range(H):
            backward_add(l, h)
            if l > 0:
                backward_partial(l - 1, h)
                send_bulk()
    send_grad_in(0)
    send_some_out(len(waiting_out))

    wait_bytes(gi_recv, g_recv)
    wait_bytes(go_recv, h_recv)
    grad_in = gin_ref[...]
    grad_out = gout_ref[...]
    for k in range(S - 1):
        grad_in = grad_in + gi_recv[k].astype(F32)
        grad_out = grad_out + go_recv[k].astype(F32)
    gin_ref[...] = grad_in
    gout_ref[...] = grad_out
    sq = jnp.sum((grad_in * grad_in).reshape(F // 8, 8, R), axis=0)
    sq_out = jnp.sum((grad_out * grad_out).reshape(R // 8, 8, F), axis=0)
    for k in range(F // 128):
        sq = sq + sq_out[:, k * 128 : (k + 1) * 128]
    sq_send[...] = sq

    def tell(j, carry):
        other = lax.rem(me + j, N)
        send(
            sq_send, sq_recv.at[pl.ds(pl.multiple_of((N - 1 - j) * 8, 8), 8), :],
            q_send, q_recv, other // DP, lax.rem(other, DP),
        )
        return carry

    lax.fori_loop(1, N, tell, 0)
    wait_bytes(sq_recv, q_recv)
    tot_ref[...] = sq + jnp.sum(sq_recv[...].reshape(N - 1, 8, 128), axis=0)

    wait_bytes(out_hbm, o_recv)
    wait_bytes(xs.at[pl.ds(0, (N - 1) * rb)], o_send)
    for h in range(H):
        wait_bytes(xs.at[head], x_send.at[h])
        wait_bytes(xs.at[head], c_send.at[h])
    wait_bytes(gains.at[pl.ds(0, S - 1)], gn_send)
    wait_bytes(wi.at[pl.ds(0, S - 1)], wi_ssem)
    wait_bytes(wo.at[pl.ds(0, S - 1)], wo_ssem)
    wait_bytes(gi_recv, g_send)
    wait_bytes(go_recv, h_send)
    wait_bytes(sq_recv, q_send)
    for k in range(S * H):
        wait_bytes(rs_f.at[k, head], pf_s.at[k])
        wait_bytes(ag_f.at[0, head], af_s.at[k])
        wait_bytes(rs_b.at[k, head], pb_s.at[k])
        wait_bytes(ag_b.at[0, head], ab_s.at[k])


def run_stack(x, cot, gain, win, wout):
    S = lax.axis_size("section")
    DP = lax.axis_size("dp")
    tok, D = x.shape
    F, R = win.shape
    rb = tok // S
    H = 2 if rb % 32 == 0 else 1
    T = DP * rb
    N = S * DP
    sem = pltpu.SemaphoreType.DMA
    any_spec = pl.BlockSpec(memory_space=pl.ANY)
    vmem_spec = pl.BlockSpec(memory_space=pltpu.VMEM)
    scratch = [
        pltpu.VMEM(((S + 1) * T, F), BF16),
        pltpu.VMEM((T, F), BF16),
        pltpu.VMEM((S, T, F), BF16),
        pltpu.VMEM((S, 1, F), F32),
        pltpu.VMEM((S, F, R), BF16),
        pltpu.VMEM((S, R, F), BF16),
        pltpu.VMEM((S * H, T // H, 2 * R), BF16),
        pltpu.VMEM((S * H, T // H, 2 * R), BF16),
        pltpu.VMEM((S, T, R), BF16),
        pltpu.VMEM((S * H, T // H, R), BF16),
        pltpu.VMEM((S * H, T // H, R), BF16),
        pltpu.VMEM((S, T, 2 * R), BF16),
        pltpu.VMEM((S * H, rb // H, R), F32),
        pltpu.VMEM((S * H, rb // H, R), F32),
        pltpu.VMEM((S * H, rb // H, R), F32),
        pltpu.VMEM((S, F, R), BF16),
        pltpu.VMEM((S, R, F), BF16),
        pltpu.VMEM((S - 1, F, R), BF16),
        pltpu.VMEM((S - 1, R, F), BF16),
        pltpu.VMEM((8, 128), F32),
        pltpu.VMEM(((N - 1) * 8, 128), F32),
        sem((H,)), sem((H,)), sem((H,)), sem((H,)), sem, sem((S,)),
        sem, sem((S,)), sem, sem((S,)),
        sem((S * H,)), sem((S * H,)), sem((S * H,)), sem((S * H,)),
        sem((S * H,)), sem((S * H,)), sem((S * H,)), sem((S * H,)),
        sem, sem, sem, sem, sem, sem, sem, sem,
    ]
    return pl.pallas_call(
        functools.partial(stack_kernel, S, DP, H, rb, F, R, D),
        out_shape=(
            jax.ShapeDtypeStruct((tok, D), BF16),
            jax.ShapeDtypeStruct((F, R), F32),
            jax.ShapeDtypeStruct((R, F), F32),
            jax.ShapeDtypeStruct((8, 128), F32),
        ),
        in_specs=[any_spec] * 3 + [vmem_spec] * 2,
        out_specs=(any_spec, vmem_spec, vmem_spec, vmem_spec),
        scratch_shapes=scratch,
        compiler_params=pltpu.CompilerParams(
            collective_id=0, has_side_effects=True, vmem_limit_bytes=56 * 1024 * 1024
        ),
        name="adapter_stack",
    )(x, cot, gain, win, wout)


def shards(
    stack_input, out_cotangent, norm_gain, master_in, master_out,
    first_in, first_out, second_in, second_out,
):
    num_sections = lax.axis_size("section")
    model_width = stack_input.shape[1]
    rank_width = master_in.shape[2]
    section_rows, shard_in, shard_out, squares = run_stack(
        stack_input, out_cotangent, norm_gain,
        master_in[0], master_out[0],
    )
    total_sq = jnp.sum(squares)
    norm_limit = clip_rms * math.sqrt(2.0 * model_width * rank_width * num_sections)
    clip_factor = norm_limit / jnp.maximum(jnp.sqrt(total_sq), norm_limit)
    new_in, new_first_in, new_second_in = adam_update(
        master_in[0], first_in[0], second_in[0], clip_factor * shard_in
    )
    new_out, new_first_out, new_second_out = adam_update(
        master_out[0], first_out[0], second_out[0], clip_factor * shard_out
    )
    return (
        section_rows[None],
        new_in[None],
        new_out[None],
        new_first_in[None],
        new_first_out[None],
        new_second_in[None],
        new_second_out[None],
    )


def solution(mesh):
    in_specs = (
        P("dp", None),
        P("dp", None),
        P("section", None),
        P("section", "dp", None),
        P("section", None, "dp"),
        P("section", "dp", None),
        P("section", None, "dp"),
        P("section", "dp", None),
        P("section", None, "dp"),
    )
    out_specs = (
        P("section", "dp", None),
        P("section", "dp", None),
        P("section", None, "dp"),
        P("section", "dp", None),
        P("section", None, "dp"),
        P("section", "dp", None),
        P("section", None, "dp"),
    )
    return jax.shard_map(shards, mesh=mesh, in_specs=in_specs, out_specs=out_specs, check_vma=False)
```

```python
import functools
import math

import jax
import jax.numpy as jnp
from jax import lax
from jax.experimental import pallas as pl
from jax.experimental.pallas import tpu as pltpu
from jax.sharding import PartitionSpec as P

STEP = 10

norm_eps = 1e-05
gelu_coef = 0.7978845608028654
beta_one = 0.9
beta_two = 0.95
adam_eps = 1e-08
learn_rate = 0.05
decay_rate = 0.1
clip_rms = 0.5

BF16 = jnp.bfloat16
F32 = jnp.float32


def gelu_pair(hidden_pre):
    inner_arg = gelu_coef * (hidden_pre + 0.044715 * hidden_pre * hidden_pre * hidden_pre)
    tangent = jnp.tanh(inner_arg)
    gelu_value = 0.5 * hidden_pre * (1.0 + tangent)
    gelu_slope = 0.5 * (1.0 + tangent) + 0.5 * hidden_pre * (
        1.0 - tangent * tangent
    ) * gelu_coef * (1.0 + 3.0 * 0.044715 * hidden_pre * hidden_pre)
    return (gelu_value, gelu_slope)


def contract_rows(left_arr, right_arr):
    return lax.dot_general(
        left_arr, right_arr, (((0,), (0,)), ((), ())), preferred_element_type=F32
    )


def contract_last(left_arr, right_arr):
    return lax.dot_general(
        left_arr, right_arr, (((1,), (1,)), ((), ())), preferred_element_type=F32
    )


def adam_update(master, first, second, grad):
    first_new = beta_one * first + (1.0 - beta_one) * grad
    second_new = beta_two * second + (1.0 - beta_two) * grad * grad
    first_hat = first_new / (1.0 - beta_one**STEP)
    second_hat = second_new / (1.0 - beta_two**STEP)
    master_new = master - learn_rate * (
        first_hat / (jnp.sqrt(second_hat) + adam_eps) + decay_rate * master
    )
    return (master_new, first_new, second_new)


def split_halves(column, width):
    high = column.astype(BF16)
    low = (column - high.astype(F32)).astype(BF16)
    shape = (column.shape[0], width)
    return jnp.concatenate(
        [jnp.broadcast_to(high, shape), jnp.broadcast_to(low, shape)], axis=1
    )


def join_halves(values, start, width):
    high = values[:, start : start + 1].astype(F32)
    return high + values[:, start + width : start + width + 1].astype(F32)


def stack_kernel(
    S, DP, H, M, rb, F, R, D,
    x_hbm, cot_hbm, gain_hbm, win_ref, wout_ref,
    out_hbm, gin_ref, gout_ref, tot_ref,
    xs, cot, delta, gains, wi, wo,
    pay_f, rs_f, ag_f, pay_b, rs_b, ag_b,
    pre_keep, sum_keep, inv_keep,
    gi_send, go_send, gi_recv, go_recv, sq_send, sq_recv,
    near_x, near_w, near_act,
    x_send, x_recv, c_send, c_recv, gn_send, gn_recv,
    wi_ssem, wi_rsem, wo_ssem, wo_rsem,
    pf_s, pf_r, af_s, af_r, pb_s, pb_r, ab_s, ab_r,
    nx_s, nx_r, nw_s, nw_r, na_s, na_r,
    o_send, o_recv, g_send, g_recv, h_send, h_recv, q_send, q_recv,
):
    q = lax.axis_index("section")
    d = lax.axis_index("dp")
    N = S * DP
    T = DP * rb
    rh = rb // H
    Th = DP * rh

    def place(sec, dp):
        return {"section": sec, "dp": dp}

    def send(src, dst, ssem, rsem, sec, dp):
        pltpu.make_async_remote_copy(
            src_ref=src, dst_ref=dst, send_sem=ssem, recv_sem=rsem,
            device_id=place(sec, dp), device_id_type=pl.DeviceIdType.MESH,
        ).start()

    def wait_bytes(ref, sem):
        pltpu.make_async_copy(ref, ref, sem).wait()

    def home_rows(h):
        return pl.ds(pl.multiple_of(q * rb + h * rh, rh), rh)

    def rows(block, h=0, base=0):
        return pl.ds(pl.multiple_of(base + h * Th + block * rh, rh), rh)

    def cols(block):
        return pl.ds(pl.multiple_of(block * F, 128), F)

    me = q * DP + d
    barrier = pltpu.get_barrier_semaphore()

    def greet(j, carry):
        other = lax.rem(me + j, N)
        pl.semaphore_signal(
            barrier, inc=1, device_id=place(other // DP, lax.rem(other, DP)),
            device_id_type=pl.DeviceIdType.MESH,
        )
        return carry

    lax.fori_loop(1, N, greet, 0)
    own_gain = pltpu.make_async_copy(gain_hbm.at[:, cols(d)], gains.at[q], gn_recv.at[q])
    own_gain.start()
    wi[q] = win_ref[...].astype(BF16)
    wo[q] = wout_ref[...].astype(BF16)
    own_gain.wait()
    pl.semaphore_wait(barrier, N - 1)

    def send_rows(h, i, src_hbm, dst, ssem, rsem):
        target = dst.at[rows(d, h), :]
        if i == 0:
            src = src_hbm.at[home_rows(h), cols(d)]
            pltpu.make_async_copy(src, target, rsem.at[h]).start()
        else:
            peer = lax.rem(d + i, DP)
            src = src_hbm.at[home_rows(h), cols(peer)]
            send(src, target, ssem.at[h], rsem.at[h], q, peer)

    def spread_layers(src, dst, ssem, rsem):
        for j in [S // 2] + [k for k in range(1, S) if k != S // 2]:
            send(src, dst.at[q], ssem, rsem.at[q], lax.rem(q + j, S), d)

    def wait_layer(buffer, rsem, l):
        @pl.when(q != l)
        def _():
            wait_bytes(buffer.at[l], rsem.at[l])

    def exchange(src_of, target, ssem, rsem):
        def body(i, carry):
            peer = lax.rem(d + i, DP)
            send(src_of(peer), target, ssem, rsem, q, peer)
            return carry

        lax.fori_loop(1, DP, body, 0)

    head = pl.ds(0, (DP - 1) * rh)

    for h in range(H):
        for i in range(DP):
            send_rows(h, i, x_hbm, xs.at[pl.ds(0, T)], x_send, x_recv)
        if h == 0:
            spread_layers(gains.at[q], gains, gn_send, gn_recv)
            spread_layers(wi.at[q], wi, wi_ssem, wi_rsem)

    def layer_rows(l):
        return pl.ds(l * T, T)

    def stream_rows(h, l=0):
        return pl.ds(l * T + h * Th, Th)

    def send_output(l, h, i):
        peer = lax.rem(d + i, DP)
        block = xs.at[rows(peer, h, (l + 1) * T), :]
        target = out_hbm.at[home_rows(h), cols(d)]
        if i > 0:
            send(block, target, o_send, o_recv, l, peer)
            return

        @pl.when(q != l)
        def _():
            send(block, target, o_send, o_recv, l, peer)

        @pl.when(q == l)
        def _():
            pltpu.make_async_copy(block, target, o_recv).start()

    near = M > 1
    tok = S * rb
    Z = DP // M
    Fs = F // S
    group = d // M
    member = lax.rem(d, M)

    def near_cols(g):
        return pl.ds(pl.multiple_of((g * M + member) * F + q * Fs, 128), Fs)

    def mate_cols(g, mate):
        return pl.ds(pl.multiple_of((g * M + mate) * F + q * Fs, 128), Fs)

    def near_rows(m):
        return pl.ds(pl.multiple_of(m * tok, tok), tok)

    def send_near_x():
        for g in range(Z):
            target = near_x.at[0, g, near_rows(member), :]
            pltpu.make_async_copy(x_hbm.at[:, near_cols(g)], target, nx_r).start()
            for j in range(1, M):
                mate = lax.rem(member + j, M)
                src = x_hbm.at[:, mate_cols(g, mate)]
                send(src, target, nx_s, nx_r, q, group * M + mate)

    def send_near_w(l, j):
        share = wo.at[l, :, pl.ds(pl.multiple_of(q * Fs, 128), Fs)]
        target = near_w.at[l, group]
        if j == 0:
            pltpu.make_async_copy(share, target, nw_r.at[l]).start()
        else:
            other = lax.rem(group + j, Z)
            send(share, target, nw_s.at[l], nw_r.at[l], q, other * M + member)

    def send_near_act(l, h, mine):
        target = near_act.at[
            l, pl.ds(pl.multiple_of(member * tok + q * rb + h * rh, rh), rh), :
        ]
        target[...] = mine[...]

        def body(j, carry):
            sec = lax.rem(q + j // M, S)
            mate = lax.rem(member + lax.rem(j, M), M)
            send(target, target, na_s.at[l], na_r.at[l], sec, group * M + mate)
            return carry

        lax.fori_loop(1, S * M, body, 0)

    def rebuild(l):
        if not near:
            return
        while waiting_w and waiting_w[0][0] <= l:
            send_near_w(*waiting_w.pop(0))
        if l == 0:
            wait_bytes(near_x.at[0], nx_r)
        wait_bytes(near_w.at[l], nw_r.at[l])
        wait_bytes(near_act.at[l, pl.ds(0, (S * M - 1) * rb), :], na_r.at[l])
        for g in range(Z):
            near_x[l + 1, g] = (
                near_x[l, g].astype(F32)
                + jnp.dot(near_act[l], near_w[l, g], preferred_element_type=F32)
            ).astype(BF16)
        waiting_out.extend((l, g, j) for g in range(Z) for j in range(M))

    def send_near_output(l, g, j):
        mate = lax.rem(member + j, M)
        block = near_x.at[l + 1, g, near_rows(mate), :]
        target = out_hbm.at[:, near_cols(g)]
        if j > 0:
            send(block, target, o_send, o_recv, l, group * M + mate)
            return

        @pl.when(q != l)
        def _():
            send(block, target, o_send, o_recv, l, d)

        @pl.when(q == l)
        def _():
            pltpu.make_async_copy(block, target, o_recv).start()

    waiting_w = []
    waiting_cot = [(h, i) for h in range(H) for i in range(DP)]
    waiting_out = []

    def send_some_cot(count):
        for _ in range(min(count, len(waiting_cot))):
            send_rows(*waiting_cot.pop(0), cot_hbm, cot, c_send, c_recv)

    def send_some_out(count):
        for _ in range(min(count, len(waiting_out))):
            (send_near_output if near else send_output)(*waiting_out.pop(0))

    def send_bulk():
        if waiting_cot:
            send_some_cot(-(-DP // S))
        elif waiting_w:
            for _ in range(min(3, len(waiting_w))):
                send_near_w(*waiting_w.pop(0))
        else:
            send_some_out(-(-DP // 3))

    def add_blocks(buffer, k):
        total = buffer[k, 0:rh, :].astype(F32)
        for b in range(1, DP):
            total = total + buffer[k, b * rh : (b + 1) * rh, :].astype(F32)
        return total

    def forward_partial(l, h):
        k = l * H + h
        if l == 0:
            wait_bytes(xs.at[stream_rows(h)], x_recv.at[h])
        if h == 0:
            wait_layer(gains, gn_recv, l)
            wait_layer(wi, wi_rsem, l)
        wide = xs[stream_rows(h, l), :].astype(F32)
        part = jnp.dot((wide * gains[l]).astype(BF16), wi[l], preferred_element_type=F32)
        squares = jnp.sum(wide * wide, axis=1, keepdims=True)
        pay_f[k] = jnp.concatenate([part.astype(BF16), split_halves(squares, R // 2)], axis=1)
        exchange(
            lambda peer: pay_f.at[k, rows(peer), :], rs_f.at[k, rows(d), :], pf_s.at[k], pf_r.at[k]
        )
        rs_f[k, rows(d), :] = pay_f[k, rows(d), :]

    def forward_act(l, h):
        k = l * H + h
        wait_bytes(rs_f.at[k, head], pf_r.at[k])
        total = add_blocks(rs_f, k)
        inv = lax.rsqrt(join_halves(total, R, R // 2) / D + norm_eps)
        pre = total[:, :R] * inv
        act, _ = gelu_pair(pre)
        mine = ag_f.at[l, rows(d, h), :]
        mine[...] = act.astype(BF16)
        exchange(lambda peer: mine, mine, af_s.at[k], af_r.at[k])
        if near:
            send_near_act(l, h, mine)
        pre_keep[k] = pre
        sum_keep[k] = total[:, :R]
        inv_keep[k] = jnp.broadcast_to(inv, (rh, R))

    def forward_add(l, h):
        k = l * H + h
        if h == 0:
            wait_layer(wo, wo_rsem, l)
            if near:
                waiting_w.extend((l, j) for j in range(Z))
        wait_bytes(ag_f.at[l, head], af_r.at[k])
        xs[stream_rows(h, l + 1), :] = (
            xs[stream_rows(h, l), :].astype(F32)
            + jnp.dot(ag_f[l, stream_rows(h), :], wo[l], preferred_element_type=F32)
        ).astype(BF16)
        if not near:
            waiting_out.extend((l, h, i) for i in range(DP))

    for h in range(H):
        forward_partial(0, h)
        if h == 0:
            spread_layers(wo.at[q], wo, wo_ssem, wo_rsem)
            if near:
                send_near_x()
        send_bulk()
    for l in range(S):
        for h in range(H):
            forward_act(l, h)
            send_bulk()
        if l > 1:
            rebuild(l - 2)
        for h in range(H):
            forward_add(l, h)
            if l + 1 < S:
                forward_partial(l + 1, h)
                send_bulk()

    send_some_cot(DP * H)

    def pass_grad(l, grad, own, outgoing, arriving, ssem, rsem):
        @pl.when(q == l)
        def _():
            own[...] = grad

        @pl.when(q != l)
        def _():
            outgoing[l] = grad.astype(BF16)
            slot = lax.rem(q - l - 1 + 2 * S, S)
            send(outgoing.at[l], arriving.at[slot], ssem, rsem, l, d)

    def send_grad_in(l):
        inv = join_halves(ag_b[l], R + R // 2, R // 4)
        normed = (xs[layer_rows(l), :].astype(F32) * inv * gains[l]).astype(BF16)
        grad_in = contract_rows(normed, ag_b[l, :, :R])
        pass_grad(l, grad_in, gin_ref, gi_send, gi_recv, g_send, g_recv)

    def send_grad_out(l, incoming):
        grad_out = contract_rows(ag_f[l], incoming[...])
        pass_grad(l, grad_out, gout_ref, go_send, go_recv, h_send, h_recv)

    def incoming(l):
        return cot if l == S - 1 else delta.at[l]

    def backward_partial(l, h):
        k = l * H + h
        if l == S - 1:
            wait_bytes(cot.at[stream_rows(h)], c_recv.at[h])
        part = contract_last(incoming(l)[stream_rows(h), :], wo[l])
        pay_b[k] = part.astype(BF16)
        exchange(
            lambda peer: pay_b.at[k, rows(peer), :], rs_b.at[k, rows(d), :], pb_s.at[k], pb_r.at[k]
        )
        rs_b[k, rows(d), :] = pay_b[k, rows(d), :]

    def backward_slope(l, h):
        k = l * H + h
        _, slope = gelu_pair(pre_keep[k])
        inv = inv_keep[k][:, 0:1]
        wait_bytes(rs_b.at[k, head], pb_r.at[k])
        d_pre = (add_blocks(rs_b, k) * slope).astype(BF16)
        mean = jnp.sum(d_pre.astype(F32) * sum_keep[k], axis=1, keepdims=True) / D
        mine = ag_b.at[l, rows(d, h), :]
        mine[...] = jnp.concatenate(
            [d_pre, split_halves(inv * inv * inv * mean, R // 4), split_halves(inv, R // 4)],
            axis=1,
        )
        exchange(lambda peer: mine, mine, ab_s.at[k], ab_r.at[k])

    def backward_add(l, h):
        wait_bytes(ag_b.at[l, head], ab_r.at[l * H + h])
        if l == 0:
            return
        gathered = ag_b[l, stream_rows(h), :]
        scaled = contract_last(gathered[:, :R], wi[l]) * gains[l]
        delta[l - 1, stream_rows(h), :] = (
            incoming(l)[stream_rows(h), :].astype(F32)
            + join_halves(gathered, R + R // 2, R // 4) * scaled
            - xs[stream_rows(h, l), :].astype(F32) * join_halves(gathered, R, R // 4)
        ).astype(BF16)

    for h in range(H):
        backward_partial(S - 1, h)
        send_bulk()
    for l in range(S - 1, -1, -1):
        send_grad_out(l, incoming(l))
        for h in range(H):
            backward_slope(l, h)
            send_bulk()
        if l + 1 < S:
            send_grad_in(l + 1)
        if l > S - 3:
            rebuild(S - 2 + S - 1 - l)
        for h in range(H):
            backward_add(l, h)
            if l > 0:
                backward_partial(l - 1, h)
                send_bulk()
    send_grad_in(0)
    send_some_out(len(waiting_out))

    wait_bytes(gi_recv, g_recv)
    wait_bytes(go_recv, h_recv)
    grad_in = gin_ref[...]
    grad_out = gout_ref[...]
    for k in range(S - 1):
        grad_in = grad_in + gi_recv[k].astype(F32)
        grad_out = grad_out + go_recv[k].astype(F32)
    gin_ref[...] = grad_in
    gout_ref[...] = grad_out
    sq = jnp.sum((grad_in * grad_in).reshape(F // 8, 8, R), axis=0)
    sq_out = jnp.sum((grad_out * grad_out).reshape(R // 8, 8, F), axis=0)
    for k in range(F // 128):
        sq = sq + sq_out[:, k * 128 : (k + 1) * 128]
    sq_send[...] = sq

    def tell(j, carry):
        other = lax.rem(me + j, N)
        send(
            sq_send, sq_recv.at[pl.ds(pl.multiple_of((N - 1 - j) * 8, 8), 8), :],
            q_send, q_recv, other // DP, lax.rem(other, DP),
        )
        return carry

    lax.fori_loop(1, N, tell, 0)
    wait_bytes(sq_recv, q_recv)
    tot_ref[...] = sq + jnp.sum(sq_recv[...].reshape(N - 1, 8, 128), axis=0)

    wait_bytes(out_hbm, o_recv)
    wait_bytes(xs.at[pl.ds(0, (N - (Z if near else 1)) * rb)], o_send)
    if near:
        wait_bytes(near_x.at[0, :, pl.ds(0, (M - 1) * tok), :], nx_s)
        for l in range(S):
            wait_bytes(near_w.at[l, pl.ds(0, Z - 1)], nw_s.at[l])
            wait_bytes(near_act.at[l, pl.ds(0, (S * M - 1) * rb), :], na_s.at[l])
    for h in range(H):
        wait_bytes(xs.at[head], x_send.at[h])
        wait_bytes(xs.at[head], c_send.at[h])
    wait_bytes(gains.at[pl.ds(0, S - 1)], gn_send)
    wait_bytes(wi.at[pl.ds(0, S - 1)], wi_ssem)
    wait_bytes(wo.at[pl.ds(0, S - 1)], wo_ssem)
    wait_bytes(gi_recv, g_send)
    wait_bytes(go_recv, h_send)
    wait_bytes(sq_recv, q_send)
    for k in range(S * H):
        wait_bytes(rs_f.at[k, head], pf_s.at[k])
        wait_bytes(ag_f.at[0, head], af_s.at[k])
        wait_bytes(rs_b.at[k, head], pb_s.at[k])
        wait_bytes(ag_b.at[0, head], ab_s.at[k])


def run_stack(x, cot, gain, win, wout):
    S = lax.axis_size("section")
    DP = lax.axis_size("dp")
    tok, D = x.shape
    F, R = win.shape
    rb = tok // S
    H = 2 if rb % 32 == 0 else 1
    M = 2 if DP % 2 == 0 and F % (128 * S) == 0 else 1
    Z = DP // M
    Fs = F // S if M > 1 else 128
    near = (S, Z, M * tok) if M > 1 else (1, 1, 16)
    T = DP * rb
    N = S * DP
    sem = pltpu.SemaphoreType.DMA
    any_spec = pl.BlockSpec(memory_space=pl.ANY)
    vmem_spec = pl.BlockSpec(memory_space=pltpu.VMEM)
    scratch = [
        pltpu.VMEM(((S + 1) * T, F), BF16),
        pltpu.VMEM((T, F), BF16),
        pltpu.VMEM((S, T, F), BF16),
        pltpu.VMEM((S, 1, F), F32),
        pltpu.VMEM((S, F, R), BF16),
        pltpu.VMEM((S, R, F), BF16),
        pltpu.VMEM((S * H, T // H, 2 * R), BF16),
        pltpu.VMEM((S * H, T // H, 2 * R), BF16),
        pltpu.VMEM((S, T, R), BF16),
        pltpu.VMEM((S * H, T // H, R), BF16),
        pltpu.VMEM((S * H, T // H, R), BF16),
        pltpu.VMEM((S, T, 2 * R), BF16),
        pltpu.VMEM((S * H, rb // H, R), F32),
        pltpu.VMEM((S * H, rb // H, R), F32),
        pltpu.VMEM((S * H, rb // H, R), F32),
        pltpu.VMEM((S, F, R), BF16),
        pltpu.VMEM((S, R, F), BF16),
        pltpu.VMEM((S - 1, F, R), BF16),
        pltpu.VMEM((S - 1, R, F), BF16),
        pltpu.VMEM((8, 128), F32),
        pltpu.VMEM(((N - 1) * 8, 128), F32),
        pltpu.VMEM((near[0] + 1, near[1], near[2], Fs), BF16),
        pltpu.VMEM((near[0], near[1], R, Fs), BF16),
        pltpu.VMEM((near[0], near[2], R), BF16),
        sem((H,)), sem((H,)), sem((H,)), sem((H,)), sem, sem((S,)),
        sem, sem((S,)), sem, sem((S,)),
        sem((S * H,)), sem((S * H,)), sem((S * H,)), sem((S * H,)),
        sem((S * H,)), sem((S * H,)), sem((S * H,)), sem((S * H,)),
        sem, sem, sem((S,)), sem((S,)), sem((S,)), sem((S,)),
        sem, sem, sem, sem, sem, sem, sem, sem,
    ]
    return pl.pallas_call(
        functools.partial(stack_kernel, S, DP, H, M, rb, F, R, D),
        out_shape=(
            jax.ShapeDtypeStruct((tok, D), BF16),
            jax.ShapeDtypeStruct((F, R), F32),
            jax.ShapeDtypeStruct((R, F), F32),
            jax.ShapeDtypeStruct((8, 128), F32),
        ),
        in_specs=[any_spec] * 3 + [vmem_spec] * 2,
        out_specs=(any_spec, vmem_spec, vmem_spec, vmem_spec),
        scratch_shapes=scratch,
        compiler_params=pltpu.CompilerParams(
            collective_id=0, has_side_effects=True, vmem_limit_bytes=56 * 1024 * 1024
        ),
        name="adapter_stack",
    )(x, cot, gain, win, wout)


def shards(
    stack_input, out_cotangent, norm_gain, master_in, master_out,
    first_in, first_out, second_in, second_out,
):
    num_sections = lax.axis_size("section")
    model_width = stack_input.shape[1]
    rank_width = master_in.shape[2]
    section_rows, shard_in, shard_out, squares = run_stack(
        stack_input, out_cotangent, norm_gain,
        master_in[0], master_out[0],
    )
    total_sq = jnp.sum(squares)
    norm_limit = clip_rms * math.sqrt(2.0 * model_width * rank_width * num_sections)
    clip_factor = norm_limit / jnp.maximum(jnp.sqrt(total_sq), norm_limit)
    new_in, new_first_in, new_second_in = adam_update(
        master_in[0], first_in[0], second_in[0], clip_factor * shard_in
    )
    new_out, new_first_out, new_second_out = adam_update(
        master_out[0], first_out[0], second_out[0], clip_factor * shard_out
    )
    return (
        section_rows[None],
        new_in[None],
        new_out[None],
        new_first_in[None],
        new_first_out[None],
        new_second_in[None],
        new_second_out[None],
    )


def solution(mesh):
    in_specs = (
        P("dp", None),
        P("dp", None),
        P("section", None),
        P("section", "dp", None),
        P("section", None, "dp"),
        P("section", "dp", None),
        P("section", None, "dp"),
        P("section", "dp", None),
        P("section", None, "dp"),
    )
    out_specs = (
        P("section", "dp", None),
        P("section", "dp", None),
        P("section", None, "dp"),
        P("section", "dp", None),
        P("section", None, "dp"),
        P("section", "dp", None),
        P("section", None, "dp"),
    )
    return jax.shard_map(shards, mesh=mesh, in_specs=in_specs, out_specs=out_specs, check_vma=False)
```

```python
import functools
import math

import jax
import jax.numpy as jnp
from jax import lax
from jax.experimental import pallas as pl
from jax.experimental.pallas import tpu as pltpu
from jax.sharding import PartitionSpec as P

STEP = 10

norm_eps = 1e-05
gelu_coef = 0.7978845608028654
beta_one = 0.9
beta_two = 0.95
adam_eps = 1e-08
learn_rate = 0.05
decay_rate = 0.1
clip_rms = 0.5

BF16 = jnp.bfloat16
F32 = jnp.float32


def gelu_pair(hidden_pre):
    inner_arg = gelu_coef * (hidden_pre + 0.044715 * hidden_pre * hidden_pre * hidden_pre)
    tangent = jnp.tanh(inner_arg)
    gelu_value = 0.5 * hidden_pre * (1.0 + tangent)
    gelu_slope = 0.5 * (1.0 + tangent) + 0.5 * hidden_pre * (
        1.0 - tangent * tangent
    ) * gelu_coef * (1.0 + 3.0 * 0.044715 * hidden_pre * hidden_pre)
    return (gelu_value, gelu_slope)


def contract_rows(left_arr, right_arr):
    return lax.dot_general(
        left_arr, right_arr, (((0,), (0,)), ((), ())), preferred_element_type=F32
    )


def contract_last(left_arr, right_arr):
    return lax.dot_general(
        left_arr, right_arr, (((1,), (1,)), ((), ())), preferred_element_type=F32
    )


def adam_update(master, first, second, grad):
    first_new = beta_one * first + (1.0 - beta_one) * grad
    second_new = beta_two * second + (1.0 - beta_two) * grad * grad
    first_hat = first_new / (1.0 - beta_one**STEP)
    second_hat = second_new / (1.0 - beta_two**STEP)
    master_new = master - learn_rate * (
        first_hat / (jnp.sqrt(second_hat) + adam_eps) + decay_rate * master
    )
    return (master_new, first_new, second_new)


def split_halves(column, width):
    high = column.astype(BF16)
    low = (column - high.astype(F32)).astype(BF16)
    shape = (column.shape[0], width)
    return jnp.concatenate(
        [jnp.broadcast_to(high, shape), jnp.broadcast_to(low, shape)], axis=1
    )


def join_halves(values, start, width):
    high = values[:, start : start + 1].astype(F32)
    return high + values[:, start + width : start + width + 1].astype(F32)


def stack_kernel(
    S, DP, H, rb, F, R, D,
    x_hbm, cot_hbm, gain_hbm, win_ref, wout_ref,
    out_hbm, gin_ref, gout_ref, tot_ref,
    xs, cot, delta, gains, wi, wo,
    pay_f, rs_f, ag_f, pay_b, rs_b, ag_b,
    pre_keep, sum_keep, inv_keep,
    gi_send, go_send, gi_recv, go_recv, sq_send, sq_recv,
    x_send, x_recv, c_send, c_recv, gn_send, gn_recv,
    wi_ssem, wi_rsem, wo_ssem, wo_rsem,
    pf_s, pf_r, af_s, af_r, pb_s, pb_r, ab_s, ab_r,
    o_send, o_recv, g_send, g_recv, h_send, h_recv, q_send, q_recv,
):
    q = lax.axis_index("section")
    d = lax.axis_index("dp")
    N = S * DP
    T = DP * rb
    rh = rb // H
    Th = DP * rh

    def place(sec, dp):
        return {"section": sec, "dp": dp}

    def send(src, dst, ssem, rsem, sec, dp):
        pltpu.make_async_remote_copy(
            src_ref=src, dst_ref=dst, send_sem=ssem, recv_sem=rsem,
            device_id=place(sec, dp), device_id_type=pl.DeviceIdType.MESH,
        ).start()

    def wait_bytes(ref, sem):
        pltpu.make_async_copy(ref, ref, sem).wait()

    def home_rows(h):
        return pl.ds(pl.multiple_of(q * rb + h * rh, rh), rh)

    def rows(block, h=0, base=0):
        return pl.ds(pl.multiple_of(base + h * Th + block * rh, rh), rh)

    def cols(block):
        return pl.ds(pl.multiple_of(block * F, 128), F)

    me = q * DP + d
    barrier = pltpu.get_barrier_semaphore()

    def greet(j, carry):
        other = lax.rem(me + j, N)
        pl.semaphore_signal(
            barrier, inc=1, device_id=place(other // DP, lax.rem(other, DP)),
            device_id_type=pl.DeviceIdType.MESH,
        )
        return carry

    lax.fori_loop(1, N, greet, 0)
    own_gain = pltpu.make_async_copy(gain_hbm.at[:, cols(d)], gains.at[q], gn_recv.at[q])
    own_gain.start()
    wi[q] = win_ref[...].astype(BF16)
    wo[q] = wout_ref[...].astype(BF16)
    own_gain.wait()
    pl.semaphore_wait(barrier, N - 1)

    def send_rows(h, i, src_hbm, dst, ssem, rsem):
        target = dst.at[rows(d, h), :]
        if i == 0:
            src = src_hbm.at[home_rows(h), cols(d)]
            pltpu.make_async_copy(src, target, rsem.at[h]).start()
        else:
            peer = lax.rem(d + i, DP)
            src = src_hbm.at[home_rows(h), cols(peer)]
            send(src, target, ssem.at[h], rsem.at[h], q, peer)

    def spread_layers(src, dst, ssem, rsem):
        for j in [S // 2] + [k for k in range(1, S) if k != S // 2]:
            send(src, dst.at[q], ssem, rsem.at[q], lax.rem(q + j, S), d)

    mate = q + 1 - 2 * lax.rem(q, 2)

    def spread_weights(buffer, ssem, rsem):
        for j in range(1, S // 2):
            send(buffer.at[q], buffer.at[q], ssem, rsem.at[q], lax.rem(q + 2 * j, S), d)
        send(buffer.at[q], buffer.at[q], ssem, rsem.at[q], mate, d)

    def hand_on(buffer, ssem, rsem):
        for j in range(1, S // 2):
            l = lax.rem(q + 2 * j, S)
            wait_bytes(buffer.at[l], rsem.at[l])
            send(buffer.at[l], buffer.at[l], ssem, rsem.at[l], mate, d)

    def wait_weights(buffer, rsem, l):
        @pl.when(lax.rem(q + l, 2) == 1)
        def _():
            wait_bytes(buffer.at[l], rsem.at[l])

    def wait_layer(buffer, rsem, l):
        @pl.when(q != l)
        def _():
            wait_bytes(buffer.at[l], rsem.at[l])

    def exchange(src_of, target, ssem, rsem):
        def body(i, carry):
            peer = lax.rem(d + i, DP)
            send(src_of(peer), target, ssem, rsem, q, peer)
            return carry

        lax.fori_loop(1, DP, body, 0)

    head = pl.ds(0, (DP - 1) * rh)

    for h in range(H):
        for i in range(DP):
            send_rows(h, i, x_hbm, xs.at[pl.ds(0, T)], x_send, x_recv)
        if h == 0:
            spread_layers(gains.at[q], gains, gn_send, gn_recv)
            spread_weights(wi, wi_ssem, wi_rsem)

    def layer_rows(l):
        return pl.ds(l * T, T)

    def stream_rows(h, l=0):
        return pl.ds(l * T + h * Th, Th)

    def send_output(l, h, i):
        peer = lax.rem(d + i, DP)
        block = xs.at[rows(peer, h, (l + 1) * T), :]
        target = out_hbm.at[home_rows(h), cols(d)]
        if i > 0:
            send(block, target, o_send, o_recv, l, peer)
            return

        @pl.when(q != l)
        def _():
            send(block, target, o_send, o_recv, l, peer)

        @pl.when(q == l)
        def _():
            pltpu.make_async_copy(block, target, o_recv).start()

    waiting_cot = [(h, i) for h in range(H) for i in range(DP)]
    waiting_out = []

    def send_some_cot(count):
        for _ in range(min(count, len(waiting_cot))):
            send_rows(*waiting_cot.pop(0), cot_hbm, cot, c_send, c_recv)

    def send_some_out(count):
        for _ in range(min(count, len(waiting_out))):
            send_output(*waiting_out.pop(0))

    def send_bulk():
        if waiting_cot:
            send_some_cot(-(-DP // S))
        else:
            send_some_out(-(-DP // 3))

    def add_blocks(buffer, k):
        total = buffer[k, 0:rh, :].astype(F32)
        for b in range(1, DP):
            total = total + buffer[k, b * rh : (b + 1) * rh, :].astype(F32)
        return total

    def forward_partial(l, h):
        k = l * H + h
        if l == 0:
            wait_bytes(xs.at[stream_rows(h)], x_recv.at[h])
        if h == 0:
            wait_layer(gains, gn_recv, l)
            wait_weights(wi, wi_rsem, l)
        wide = xs[stream_rows(h, l), :].astype(F32)
        part = jnp.dot((wide * gains[l]).astype(BF16), wi[l], preferred_element_type=F32)
        squares = jnp.sum(wide * wide, axis=1, keepdims=True)
        pay_f[k] = jnp.concatenate([part.astype(BF16), split_halves(squares, R // 2)], axis=1)
        exchange(
            lambda peer: pay_f.at[k, rows(peer), :], rs_f.at[k, rows(d), :], pf_s.at[k], pf_r.at[k]
        )
        rs_f[k, rows(d), :] = pay_f[k, rows(d), :]

    def forward_act(l, h):
        k = l * H + h
        wait_bytes(rs_f.at[k, head], pf_r.at[k])
        total = add_blocks(rs_f, k)
        inv = lax.rsqrt(join_halves(total, R, R // 2) / D + norm_eps)
        pre = total[:, :R] * inv
        act, _ = gelu_pair(pre)
        mine = ag_f.at[l, rows(d, h), :]
        mine[...] = act.astype(BF16)
        exchange(lambda peer: mine, mine, af_s.at[k], af_r.at[k])
        pre_keep[k] = pre
        sum_keep[k] = total[:, :R]
        inv_keep[k] = jnp.broadcast_to(inv, (rh, R))

    def forward_add(l, h):
        k = l * H + h
        if h == 0:
            wait_weights(wo, wo_rsem, l)
        wait_bytes(ag_f.at[l, head], af_r.at[k])
        xs[stream_rows(h, l + 1), :] = (
            xs[stream_rows(h, l), :].astype(F32)
            + jnp.dot(ag_f[l, stream_rows(h), :], wo[l], preferred_element_type=F32)
        ).astype(BF16)
        waiting_out.extend((l, h, i) for i in range(DP))

    spread_weights(wo, wo_ssem, wo_rsem)
    hand_on(wi, wi_ssem, wi_rsem)
    for h in range(H):
        forward_partial(0, h)
        send_bulk()
    hand_on(wo, wo_ssem, wo_rsem)
    for l in range(S):
        for h in range(H):
            forward_act(l, h)
            send_bulk()
        for h in range(H):
            forward_add(l, h)
            if l + 1 < S:
                forward_partial(l + 1, h)
                send_bulk()

    send_some_cot(DP * H)

    def pass_grad(l, grad, own, outgoing, arriving, ssem, rsem):
        @pl.when(q == l)
        def _():
            own[...] = grad

        @pl.when(q != l)
        def _():
            outgoing[l] = grad.astype(BF16)
            slot = lax.rem(q - l - 1 + 2 * S, S)
            send(outgoing.at[l], arriving.at[slot], ssem, rsem, l, d)

    def send_grad_in(l):
        inv = join_halves(ag_b[l], R + R // 2, R // 4)
        normed = (xs[layer_rows(l), :].astype(F32) * inv * gains[l]).astype(BF16)
        grad_in = contract_rows(normed, ag_b[l, :, :R])
        pass_grad(l, grad_in, gin_ref, gi_send, gi_recv, g_send, g_recv)

    def send_grad_out(l, incoming):
        grad_out = contract_rows(ag_f[l], incoming[...])
        pass_grad(l, grad_out, gout_ref, go_send, go_recv, h_send, h_recv)

    def incoming(l):
        return cot if l == S - 1 else delta.at[l]

    def backward_partial(l, h):
        k = l * H + h
        if l == S - 1:
            wait_bytes(cot.at[stream_rows(h)], c_recv.at[h])
        part = contract_last(incoming(l)[stream_rows(h), :], wo[l])
        pay_b[k] = part.astype(BF16)
        exchange(
            lambda peer: pay_b.at[k, rows(peer), :], rs_b.at[k, rows(d), :], pb_s.at[k], pb_r.at[k]
        )
        rs_b[k, rows(d), :] = pay_b[k, rows(d), :]

    def backward_slope(l, h):
        k = l * H + h
        _, slope = gelu_pair(pre_keep[k])
        inv = inv_keep[k][:, 0:1]
        wait_bytes(rs_b.at[k, head], pb_r.at[k])
        d_pre = (add_blocks(rs_b, k) * slope).astype(BF16)
        mean = jnp.sum(d_pre.astype(F32) * sum_keep[k], axis=1, keepdims=True) / D
        mine = ag_b.at[l, rows(d, h), :]
        mine[...] = jnp.concatenate(
            [d_pre, split_halves(inv * inv * inv * mean, R // 4), split_halves(inv, R // 4)],
            axis=1,
        )
        exchange(lambda peer: mine, mine, ab_s.at[k], ab_r.at[k])

    def backward_add(l, h):
        wait_bytes(ag_b.at[l, head], ab_r.at[l * H + h])
        if l == 0:
            return
        gathered = ag_b[l, stream_rows(h), :]
        scaled = contract_last(gathered[:, :R], wi[l]) * gains[l]
        delta[l - 1, stream_rows(h), :] = (
            incoming(l)[stream_rows(h), :].astype(F32)
            + join_halves(gathered, R + R // 2, R // 4) * scaled
            - xs[stream_rows(h, l), :].astype(F32) * join_halves(gathered, R, R // 4)
        ).astype(BF16)

    for h in range(H):
        backward_partial(S - 1, h)
        send_bulk()
    for l in range(S - 1, -1, -1):
        send_grad_out(l, incoming(l))
        for h in range(H):
            backward_slope(l, h)
            send_bulk()
        if l + 1 < S:
            send_grad_in(l + 1)
        for h in range(H):
            backward_add(l, h)
            if l > 0:
                backward_partial(l - 1, h)
                send_bulk()
    send_grad_in(0)
    send_some_out(len(waiting_out))

    wait_bytes(gi_recv, g_recv)
    wait_bytes(go_recv, h_recv)
    grad_in = gin_ref[...]
    grad_out = gout_ref[...]
    for k in range(S - 1):
        grad_in = grad_in + gi_recv[k].astype(F32)
        grad_out = grad_out + go_recv[k].astype(F32)
    gin_ref[...] = grad_in
    gout_ref[...] = grad_out
    sq = jnp.sum((grad_in * grad_in).reshape(F // 8, 8, R), axis=0)
    sq_out = jnp.sum((grad_out * grad_out).reshape(R // 8, 8, F), axis=0)
    for k in range(F // 128):
        sq = sq + sq_out[:, k * 128 : (k + 1) * 128]
    sq_send[...] = sq

    def tell(j, carry):
        other = lax.rem(me + j, N)
        send(
            sq_send, sq_recv.at[pl.ds(pl.multiple_of((N - 1 - j) * 8, 8), 8), :],
            q_send, q_recv, other // DP, lax.rem(other, DP),
        )
        return carry

    lax.fori_loop(1, N, tell, 0)
    wait_bytes(sq_recv, q_recv)
    tot_ref[...] = sq + jnp.sum(sq_recv[...].reshape(N - 1, 8, 128), axis=0)

    wait_bytes(out_hbm, o_recv)
    wait_bytes(xs.at[pl.ds(0, (N - 1) * rb)], o_send)
    for h in range(H):
        wait_bytes(xs.at[head], x_send.at[h])
        wait_bytes(xs.at[head], c_send.at[h])
    wait_bytes(gains.at[pl.ds(0, S - 1)], gn_send)
    wait_bytes(wi.at[pl.ds(0, S - 1)], wi_ssem)
    wait_bytes(wo.at[pl.ds(0, S - 1)], wo_ssem)
    wait_bytes(gi_recv, g_send)
    wait_bytes(go_recv, h_send)
    wait_bytes(sq_recv, q_send)
    for k in range(S * H):
        wait_bytes(rs_f.at[k, head], pf_s.at[k])
        wait_bytes(ag_f.at[0, head], af_s.at[k])
        wait_bytes(rs_b.at[k, head], pb_s.at[k])
        wait_bytes(ag_b.at[0, head], ab_s.at[k])


def run_stack(x, cot, gain, win, wout):
    S = lax.axis_size("section")
    DP = lax.axis_size("dp")
    tok, D = x.shape
    F, R = win.shape
    rb = tok // S
    H = 2 if rb % 32 == 0 else 1
    T = DP * rb
    N = S * DP
    sem = pltpu.SemaphoreType.DMA
    any_spec = pl.BlockSpec(memory_space=pl.ANY)
    vmem_spec = pl.BlockSpec(memory_space=pltpu.VMEM)
    scratch = [
        pltpu.VMEM(((S + 1) * T, F), BF16),
        pltpu.VMEM((T, F), BF16),
        pltpu.VMEM((S, T, F), BF16),
        pltpu.VMEM((S, 1, F), F32),
        pltpu.VMEM((S, F, R), BF16),
        pltpu.VMEM((S, R, F), BF16),
        pltpu.VMEM((S * H, T // H, 2 * R), BF16),
        pltpu.VMEM((S * H, T // H, 2 * R), BF16),
        pltpu.VMEM((S, T, R), BF16),
        pltpu.VMEM((S * H, T // H, R), BF16),
        pltpu.VMEM((S * H, T // H, R), BF16),
        pltpu.VMEM((S, T, 2 * R), BF16),
        pltpu.VMEM((S * H, rb // H, R), F32),
        pltpu.VMEM((S * H, rb // H, R), F32),
        pltpu.VMEM((S * H, rb // H, R), F32),
        pltpu.VMEM((S, F, R), BF16),
        pltpu.VMEM((S, R, F), BF16),
        pltpu.VMEM((S - 1, F, R), BF16),
        pltpu.VMEM((S - 1, R, F), BF16),
        pltpu.VMEM((8, 128), F32),
        pltpu.VMEM(((N - 1) * 8, 128), F32),
        sem((H,)), sem((H,)), sem((H,)), sem((H,)), sem, sem((S,)),
        sem, sem((S,)), sem, sem((S,)),
        sem((S * H,)), sem((S * H,)), sem((S * H,)), sem((S * H,)),
        sem((S * H,)), sem((S * H,)), sem((S * H,)), sem((S * H,)),
        sem, sem, sem, sem, sem, sem, sem, sem,
    ]
    return pl.pallas_call(
        functools.partial(stack_kernel, S, DP, H, rb, F, R, D),
        out_shape=(
            jax.ShapeDtypeStruct((tok, D), BF16),
            jax.ShapeDtypeStruct((F, R), F32),
            jax.ShapeDtypeStruct((R, F), F32),
            jax.ShapeDtypeStruct((8, 128), F32),
        ),
        in_specs=[any_spec] * 3 + [vmem_spec] * 2,
        out_specs=(any_spec, vmem_spec, vmem_spec, vmem_spec),
        scratch_shapes=scratch,
        compiler_params=pltpu.CompilerParams(
            collective_id=0, has_side_effects=True, vmem_limit_bytes=56 * 1024 * 1024
        ),
        name="adapter_stack",
    )(x, cot, gain, win, wout)


def shards(
    stack_input, out_cotangent, norm_gain, master_in, master_out,
    first_in, first_out, second_in, second_out,
):
    num_sections = lax.axis_size("section")
    model_width = stack_input.shape[1]
    rank_width = master_in.shape[2]
    section_rows, shard_in, shard_out, squares = run_stack(
        stack_input, out_cotangent, norm_gain,
        master_in[0], master_out[0],
    )
    total_sq = jnp.sum(squares)
    norm_limit = clip_rms * math.sqrt(2.0 * model_width * rank_width * num_sections)
    clip_factor = norm_limit / jnp.maximum(jnp.sqrt(total_sq), norm_limit)
    new_in, new_first_in, new_second_in = adam_update(
        master_in[0], first_in[0], second_in[0], clip_factor * shard_in
    )
    new_out, new_first_out, new_second_out = adam_update(
        master_out[0], first_out[0], second_out[0], clip_factor * shard_out
    )
    return (
        section_rows[None],
        new_in[None],
        new_out[None],
        new_first_in[None],
        new_first_out[None],
        new_second_in[None],
        new_second_out[None],
    )


def solution(mesh):
    in_specs = (
        P("dp", None),
        P("dp", None),
        P("section", None),
        P("section", "dp", None),
        P("section", None, "dp"),
        P("section", "dp", None),
        P("section", None, "dp"),
        P("section", "dp", None),
        P("section", None, "dp"),
    )
    out_specs = (
        P("section", "dp", None),
        P("section", "dp", None),
        P("section", None, "dp"),
        P("section", "dp", None),
        P("section", None, "dp"),
        P("section", "dp", None),
        P("section", None, "dp"),
    )
    return jax.shard_map(shards, mesh=mesh, in_specs=in_specs, out_specs=out_specs, check_vma=False)
```

```python
import functools
import math

import jax
import jax.numpy as jnp
from jax import lax
from jax.experimental import pallas as pl
from jax.experimental.pallas import tpu as pltpu
from jax.sharding import PartitionSpec as P

STEP = 10

norm_eps = 1e-05
gelu_coef = 0.7978845608028654
beta_one = 0.9
beta_two = 0.95
adam_eps = 1e-08
learn_rate = 0.05
decay_rate = 0.1
clip_rms = 0.5

BF16 = jnp.bfloat16
F32 = jnp.float32


def gelu_pair(hidden_pre):
    inner_arg = gelu_coef * (hidden_pre + 0.044715 * hidden_pre * hidden_pre * hidden_pre)
    tangent = jnp.tanh(inner_arg)
    gelu_value = 0.5 * hidden_pre * (1.0 + tangent)
    gelu_slope = 0.5 * (1.0 + tangent) + 0.5 * hidden_pre * (
        1.0 - tangent * tangent
    ) * gelu_coef * (1.0 + 3.0 * 0.044715 * hidden_pre * hidden_pre)
    return (gelu_value, gelu_slope)


def contract_rows(left_arr, right_arr):
    return lax.dot_general(
        left_arr, right_arr, (((0,), (0,)), ((), ())), preferred_element_type=F32
    )


def contract_last(left_arr, right_arr):
    return lax.dot_general(
        left_arr, right_arr, (((1,), (1,)), ((), ())), preferred_element_type=F32
    )


def adam_update(master, first, second, grad):
    first_new = beta_one * first + (1.0 - beta_one) * grad
    second_new = beta_two * second + (1.0 - beta_two) * grad * grad
    first_hat = first_new / (1.0 - beta_one**STEP)
    second_hat = second_new / (1.0 - beta_two**STEP)
    master_new = master - learn_rate * (
        first_hat / (jnp.sqrt(second_hat) + adam_eps) + decay_rate * master
    )
    return (master_new, first_new, second_new)


def split_halves(column, width):
    high = column.astype(BF16)
    low = (column - high.astype(F32)).astype(BF16)
    shape = (column.shape[0], width)
    return jnp.concatenate(
        [jnp.broadcast_to(high, shape), jnp.broadcast_to(low, shape)], axis=1
    )


def join_halves(values, start, width):
    high = values[:, start : start + 1].astype(F32)
    return high + values[:, start + width : start + width + 1].astype(F32)


def stack_kernel(
    S, DP, H, rb, F, R, D,
    x_hbm, cot_hbm, gain_hbm, win_ref, wout_ref,
    out_hbm, gin_ref, gout_ref, tot_ref,
    xs, cot, delta, gains, wi, wo,
    pay_f, rs_f, ag_f, pay_b, rs_b, ag_b,
    pre_keep, sum_keep, inv_keep,
    gi_send, go_send, gi_recv, go_recv, sq_send, sq_recv,
    x_send, x_recv, c_send, c_recv, gn_send, gn_recv,
    wi_ssem, wi_rsem, wo_ssem, wo_rsem,
    pf_s, pf_r, af_s, af_r, pb_s, pb_r, ab_s, ab_r,
    o_send, o_recv, g_send, g_recv, h_send, h_recv, q_send, q_recv,
):
    q = lax.axis_index("section")
    d = lax.axis_index("dp")
    N = S * DP
    T = DP * rb
    rh = rb // H
    Th = DP * rh

    def place(sec, dp):
        return {"section": sec, "dp": dp}

    def send(src, dst, ssem, rsem, sec, dp):
        pltpu.make_async_remote_copy(
            src_ref=src, dst_ref=dst, send_sem=ssem, recv_sem=rsem,
            device_id=place(sec, dp), device_id_type=pl.DeviceIdType.MESH,
        ).start()

    def wait_bytes(ref, sem):
        pltpu.make_async_copy(ref, ref, sem).wait()

    def home_rows(h):
        return pl.ds(pl.multiple_of(q * rb + h * rh, rh), rh)

    def rows(block, h=0, base=0):
        return pl.ds(pl.multiple_of(base + h * Th + block * rh, rh), rh)

    def cols(block):
        return pl.ds(pl.multiple_of(block * F, 128), F)

    me = q * DP + d
    barrier = pltpu.get_barrier_semaphore()

    def greet(j, carry):
        other = lax.rem(me + j, N)
        pl.semaphore_signal(
            barrier, inc=1, device_id=place(other // DP, lax.rem(other, DP)),
            device_id_type=pl.DeviceIdType.MESH,
        )
        return carry

    lax.fori_loop(1, N, greet, 0)
    own_gain = pltpu.make_async_copy(gain_hbm.at[:, cols(d)], gains.at[q], gn_recv.at[q])
    own_gain.start()
    wi[q] = win_ref[...].astype(BF16)
    wo[q] = wout_ref[...].astype(BF16)
    own_gain.wait()
    pl.semaphore_wait(barrier, N - 1)

    def send_rows(h, i, src_hbm, dst, ssem, rsem):
        target = dst.at[rows(d, h), :]
        if i == 0:
            src = src_hbm.at[home_rows(h), cols(d)]
            pltpu.make_async_copy(src, target, rsem.at[h]).start()
        else:
            peer = lax.rem(d + i, DP)
            src = src_hbm.at[home_rows(h), cols(peer)]
            send(src, target, ssem.at[h], rsem.at[h], q, peer)

    def spread_layers(src, dst, ssem, rsem):
        for j in [S // 2] + [k for k in range(1, S) if k != S // 2]:
            send(src, dst.at[q], ssem, rsem.at[q], lax.rem(q + j, S), d)

    def wait_layer(buffer, rsem, l):
        @pl.when(q != l)
        def _():
            wait_bytes(buffer.at[l], rsem.at[l])

    def exchange(src_of, target, ssem, rsem):
        def body(i, carry):
            peer = lax.rem(d + i, DP)
            send(src_of(peer), target, ssem, rsem, q, peer)
            return carry

        lax.fori_loop(1, DP, body, 0, unroll=DP <= 8)

    head = pl.ds(0, (DP - 1) * rh)

    for h in range(H):
        for i in range(DP):
            send_rows(h, i, x_hbm, xs.at[pl.ds(0, T)], x_send, x_recv)
        if h == 0:
            spread_layers(gains.at[q], gains, gn_send, gn_recv)
            spread_layers(wi.at[q], wi, wi_ssem, wi_rsem)

    def layer_rows(l):
        return pl.ds(l * T, T)

    def stream_rows(h, l=0):
        return pl.ds(l * T + h * Th, Th)

    def send_output(l, h, i):
        peer = lax.rem(d + i, DP)
        block = xs.at[rows(peer, h, (l + 1) * T), :]
        target = out_hbm.at[home_rows(h), cols(d)]
        if i > 0:
            send(block, target, o_send, o_recv, l, peer)
            return

        @pl.when(q != l)
        def _():
            send(block, target, o_send, o_recv, l, peer)

        @pl.when(q == l)
        def _():
            pltpu.make_async_copy(block, target, o_recv).start()

    waiting_cot = [(h, i) for h in range(H) for i in range(DP)]
    waiting_out = []

    def send_some_cot(count):
        for _ in range(min(count, len(waiting_cot))):
            send_rows(*waiting_cot.pop(0), cot_hbm, cot, c_send, c_recv)

    def send_some_out(count):
        for _ in range(min(count, len(waiting_out))):
            send_output(*waiting_out.pop(0))

    def send_bulk():
        if waiting_cot:
            send_some_cot(-(-DP // S))
        else:
            send_some_out(-(-DP // 3))

    def add_blocks(buffer, k):
        total = buffer[k, 0:rh, :].astype(F32)
        for b in range(1, DP):
            total = total + buffer[k, b * rh : (b + 1) * rh, :].astype(F32)
        return total

    def forward_partial(l, h):
        k = l * H + h
        if l == 0:
            wait_bytes(xs.at[stream_rows(h)], x_recv.at[h])
        if h == 0:
            wait_layer(gains, gn_recv, l)
            wait_layer(wi, wi_rsem, l)
        wide = xs[stream_rows(h, l), :].astype(F32)
        part = jnp.dot((wide * gains[l]).astype(BF16), wi[l], preferred_element_type=F32)
        squares = jnp.sum(wide * wide, axis=1, keepdims=True)
        pay_f[k] = jnp.concatenate([part.astype(BF16), split_halves(squares, R // 2)], axis=1)
        exchange(
            lambda peer: pay_f.at[k, rows(peer), :], rs_f.at[k, rows(d), :], pf_s.at[k], pf_r.at[k]
        )
        rs_f[k, rows(d), :] = pay_f[k, rows(d), :]

    def forward_act(l, h):
        k = l * H + h
        wait_bytes(rs_f.at[k, head], pf_r.at[k])
        total = add_blocks(rs_f, k)
        inv = lax.rsqrt(join_halves(total, R, R // 2) / D + norm_eps)
        pre = total[:, :R] * inv
        act, _ = gelu_pair(pre)
        mine = ag_f.at[l, rows(d, h), :]
        mine[...] = act.astype(BF16)
        exchange(lambda peer: mine, mine, af_s.at[k], af_r.at[k])
        pre_keep[k] = pre
        sum_keep[k] = total[:, :R]
        inv_keep[k] = jnp.broadcast_to(inv, (rh, R))

    def forward_add(l, h):
        k = l * H + h
        if h == 0:
            wait_layer(wo, wo_rsem, l)
        wait_bytes(ag_f.at[l, head], af_r.at[k])
        xs[stream_rows(h, l + 1), :] = (
            xs[stream_rows(h, l), :].astype(F32)
            + jnp.dot(ag_f[l, stream_rows(h), :], wo[l], preferred_element_type=F32)
        ).astype(BF16)
        waiting_out.extend((l, h, i) for i in range(DP))

    for h in range(H):
        forward_partial(0, h)
        if h == 0:
            spread_layers(wo.at[q], wo, wo_ssem, wo_rsem)
        send_bulk()
    for l in range(S):
        for h in range(H):
            forward_act(l, h)
            send_bulk()
        for h in range(H):
            forward_add(l, h)
            if l + 1 < S:
                forward_partial(l + 1, h)
                send_bulk()

    send_some_cot(DP * H)

    def pass_grad(l, grad, own, outgoing, arriving, ssem, rsem):
        @pl.when(q == l)
        def _():
            own[...] = grad

        @pl.when(q != l)
        def _():
            outgoing[l] = grad.astype(BF16)
            slot = lax.rem(q - l - 1 + 2 * S, S)
            send(outgoing.at[l], arriving.at[slot], ssem, rsem, l, d)

    def send_grad_in(l):
        inv = join_halves(ag_b[l], R + R // 2, R // 4)
        normed = (xs[layer_rows(l), :].astype(F32) * inv * gains[l]).astype(BF16)
        grad_in = contract_rows(normed, ag_b[l, :, :R])
        pass_grad(l, grad_in, gin_ref, gi_send, gi_recv, g_send, g_recv)

    def send_grad_out(l, incoming):
        grad_out = contract_rows(ag_f[l], incoming[...])
        pass_grad(l, grad_out, gout_ref, go_send, go_recv, h_send, h_recv)

    def incoming(l):
        return cot if l == S - 1 else delta.at[l]

    def backward_partial(l, h):
        k = l * H + h
        if l == S - 1:
            wait_bytes(cot.at[stream_rows(h)], c_recv.at[h])
        part = contract_last(incoming(l)[stream_rows(h), :], wo[l])
        pay_b[k] = part.astype(BF16)
        exchange(
            lambda peer: pay_b.at[k, rows(peer), :], rs_b.at[k, rows(d), :], pb_s.at[k], pb_r.at[k]
        )
        rs_b[k, rows(d), :] = pay_b[k, rows(d), :]

    def backward_slope(l, h):
        k = l * H + h
        _, slope = gelu_pair(pre_keep[k])
        inv = inv_keep[k][:, 0:1]
        wait_bytes(rs_b.at[k, head], pb_r.at[k])
        d_pre = (add_blocks(rs_b, k) * slope).astype(BF16)
        mean = jnp.sum(d_pre.astype(F32) * sum_keep[k], axis=1, keepdims=True) / D
        mine = ag_b.at[l, rows(d, h), :]
        mine[...] = jnp.concatenate(
            [d_pre, split_halves(inv * inv * inv * mean, R // 4), split_halves(inv, R // 4)],
            axis=1,
        )
        exchange(lambda peer: mine, mine, ab_s.at[k], ab_r.at[k])

    def backward_add(l, h):
        wait_bytes(ag_b.at[l, head], ab_r.at[l * H + h])
        if l == 0:
            return
        gathered = ag_b[l, stream_rows(h), :]
        scaled = contract_last(gathered[:, :R], wi[l]) * gains[l]
        delta[l - 1, stream_rows(h), :] = (
            incoming(l)[stream_rows(h), :].astype(F32)
            + join_halves(gathered, R + R // 2, R // 4) * scaled
            - xs[stream_rows(h, l), :].astype(F32) * join_halves(gathered, R, R // 4)
        ).astype(BF16)

    for h in range(H):
        backward_partial(S - 1, h)
        send_bulk()
    for l in range(S - 1, -1, -1):
        send_grad_out(l, incoming(l))
        for h in range(H):
            backward_slope(l, h)
            send_bulk()
        if l + 1 < S:
            send_grad_in(l + 1)
        for h in range(H):
            backward_add(l, h)
            if l > 0:
                backward_partial(l - 1, h)
                send_bulk()
    send_grad_in(0)
    send_some_out(len(waiting_out))

    wait_bytes(gi_recv, g_recv)
    wait_bytes(go_recv, h_recv)
    grad_in = gin_ref[...]
    grad_out = gout_ref[...]
    for k in range(S - 1):
        grad_in = grad_in + gi_recv[k].astype(F32)
        grad_out = grad_out + go_recv[k].astype(F32)
    gin_ref[...] = grad_in
    gout_ref[...] = grad_out
    sq = jnp.sum((grad_in * grad_in).reshape(F // 8, 8, R), axis=0)
    sq_out = jnp.sum((grad_out * grad_out).reshape(R // 8, 8, F), axis=0)
    for k in range(F // 128):
        sq = sq + sq_out[:, k * 128 : (k + 1) * 128]
    sq_send[...] = sq

    def tell(j, carry):
        other = lax.rem(me + j, N)
        send(
            sq_send, sq_recv.at[pl.ds(pl.multiple_of((N - 1 - j) * 8, 8), 8), :],
            q_send, q_recv, other // DP, lax.rem(other, DP),
        )
        return carry

    lax.fori_loop(1, N, tell, 0)
    wait_bytes(sq_recv, q_recv)
    tot_ref[...] = sq + jnp.sum(sq_recv[...].reshape(N - 1, 8, 128), axis=0)

    wait_bytes(out_hbm, o_recv)
    wait_bytes(xs.at[pl.ds(0, (N - 1) * rb)], o_send)
    for h in range(H):
        wait_bytes(xs.at[head], x_send.at[h])
        wait_bytes(xs.at[head], c_send.at[h])
    wait_bytes(gains.at[pl.ds(0, S - 1)], gn_send)
    wait_bytes(wi.at[pl.ds(0, S - 1)], wi_ssem)
    wait_bytes(wo.at[pl.ds(0, S - 1)], wo_ssem)
    wait_bytes(gi_recv, g_send)
    wait_bytes(go_recv, h_send)
    wait_bytes(sq_recv, q_send)
    for k in range(S * H):
        wait_bytes(rs_f.at[k, head], pf_s.at[k])
        wait_bytes(ag_f.at[0, head], af_s.at[k])
        wait_bytes(rs_b.at[k, head], pb_s.at[k])
        wait_bytes(ag_b.at[0, head], ab_s.at[k])


def run_stack(x, cot, gain, win, wout):
    S = lax.axis_size("section")
    DP = lax.axis_size("dp")
    tok, D = x.shape
    F, R = win.shape
    rb = tok // S
    H = 2 if rb % 32 == 0 else 1
    T = DP * rb
    N = S * DP
    sem = pltpu.SemaphoreType.DMA
    any_spec = pl.BlockSpec(memory_space=pl.ANY)
    vmem_spec = pl.BlockSpec(memory_space=pltpu.VMEM)
    scratch = [
        pltpu.VMEM(((S + 1) * T, F), BF16),
        pltpu.VMEM((T, F), BF16),
        pltpu.VMEM((S, T, F), BF16),
        pltpu.VMEM((S, 1, F), F32),
        pltpu.VMEM((S, F, R), BF16),
        pltpu.VMEM((S, R, F), BF16),
        pltpu.VMEM((S * H, T // H, 2 * R), BF16),
        pltpu.VMEM((S * H, T // H, 2 * R), BF16),
        pltpu.VMEM((S, T, R), BF16),
        pltpu.VMEM((S * H, T // H, R), BF16),
        pltpu.VMEM((S * H, T // H, R), BF16),
        pltpu.VMEM((S, T, 2 * R), BF16),
        pltpu.VMEM((S * H, rb // H, R), F32),
        pltpu.VMEM((S * H, rb // H, R), F32),
        pltpu.VMEM((S * H, rb // H, R), F32),
        pltpu.VMEM((S, F, R), BF16),
        pltpu.VMEM((S, R, F), BF16),
        pltpu.VMEM((S - 1, F, R), BF16),
        pltpu.VMEM((S - 1, R, F), BF16),
        pltpu.VMEM((8, 128), F32),
        pltpu.VMEM(((N - 1) * 8, 128), F32),
        sem((H,)), sem((H,)), sem((H,)), sem((H,)), sem, sem((S,)),
        sem, sem((S,)), sem, sem((S,)),
        sem((S * H,)), sem((S * H,)), sem((S * H,)), sem((S * H,)),
        sem((S * H,)), sem((S * H,)), sem((S * H,)), sem((S * H,)),
        sem, sem, sem, sem, sem, sem, sem, sem,
    ]
    return pl.pallas_call(
        functools.partial(stack_kernel, S, DP, H, rb, F, R, D),
        out_shape=(
            jax.ShapeDtypeStruct((tok, D), BF16),
            jax.ShapeDtypeStruct((F, R), F32),
            jax.ShapeDtypeStruct((R, F), F32),
            jax.ShapeDtypeStruct((8, 128), F32),
        ),
        in_specs=[any_spec] * 3 + [vmem_spec] * 2,
        out_specs=(any_spec, vmem_spec, vmem_spec, vmem_spec),
        scratch_shapes=scratch,
        compiler_params=pltpu.CompilerParams(
            collective_id=0, has_side_effects=True, vmem_limit_bytes=56 * 1024 * 1024
        ),
        name="adapter_stack",
    )(x, cot, gain, win, wout)


def shards(
    stack_input, out_cotangent, norm_gain, master_in, master_out,
    first_in, first_out, second_in, second_out,
):
    num_sections = lax.axis_size("section")
    model_width = stack_input.shape[1]
    rank_width = master_in.shape[2]
    section_rows, shard_in, shard_out, squares = run_stack(
        stack_input, out_cotangent, norm_gain,
        master_in[0], master_out[0],
    )
    total_sq = jnp.sum(squares)
    norm_limit = clip_rms * math.sqrt(2.0 * model_width * rank_width * num_sections)
    clip_factor = norm_limit / jnp.maximum(jnp.sqrt(total_sq), norm_limit)
    new_in, new_first_in, new_second_in = adam_update(
        master_in[0], first_in[0], second_in[0], clip_factor * shard_in
    )
    new_out, new_first_out, new_second_out = adam_update(
        master_out[0], first_out[0], second_out[0], clip_factor * shard_out
    )
    return (
        section_rows[None],
        new_in[None],
        new_out[None],
        new_first_in[None],
        new_first_out[None],
        new_second_in[None],
        new_second_out[None],
    )


def solution(mesh):
    in_specs = (
        P("dp", None),
        P("dp", None),
        P("section", None),
        P("section", "dp", None),
        P("section", None, "dp"),
        P("section", "dp", None),
        P("section", None, "dp"),
        P("section", "dp", None),
        P("section", None, "dp"),
    )
    out_specs = (
        P("section", "dp", None),
        P("section", "dp", None),
        P("section", None, "dp"),
        P("section", "dp", None),
        P("section", None, "dp"),
        P("section", "dp", None),
        P("section", None, "dp"),
    )
    return jax.shard_map(shards, mesh=mesh, in_specs=in_specs, out_specs=out_specs, check_vma=False)
```
